512 devices in a mesh: gz: 32 (over y_hi, z), gy: 8 (over y_lo, x), gx: 2 (over core).
Axes of the slice: x: 4, y: 8 (y_hi: 4, y_lo: 2; y = y_hi * 2 + y_lo), z: 8, core: 2. Of those that a mesh axis runs over, the one named last changes fastest.
Arguments:
- tokens: bfloat16 [128, 64, 32, 192], P('gz', 'gy', 'gx'), may hold values from -4.5 to 4.5
- layer_norm_gain: float32 [192], replicated, may hold values from 0.25 to 1.75
- layer_norm_bias: float32 [192], replicated, may hold values from -3 to 3
- qkv_weight: bfloat16 [192, 576], replicated, may hold values from -3 to 3
- qkv_bias: float32 [576], replicated, may hold values from -3 to 3
- proj_weight: bfloat16 [192, 192], replicated, may hold values from -0.4375 to 0.4375
- bias_table: float32 [6, 1575], replicated, may hold values from -4 to 4
- grad_out: bfloat16 [128, 64, 32, 192], P('gz', 'gy', 'gx'), may hold values from -9 to 9
Outputs:
- grad_tokens: bfloat16 [128, 64, 32, 192], P('gz', 'gy', 'gx')
- grad_ln_gain: float32 [192], replicated
- grad_ln_shift: float32 [192], replicated
- grad_qkv_weight: float32 [192, 576], replicated
- grad_qkv_bias: float32 [576], replicated
- grad_proj_weight: float32 [192, 192], replicated
- grad_table: float32 [6, 1575], replicated
The draws below stay inside these ranges and needn't reach their ends.
All inputs are finite; a program needn't handle non-finite values.
Results may differ from the reference program's by a relative error of at most 0.019.
The reference program's roundings to bfloat16 on the way count: a program that leaves them out, or rounds other values in their place, can miss the bound.
Values may be sent and summed in bfloat16 or wider, within the bound.
No kernel may reach another device: no remote copies, remote signals or barrier semaphores. Data moves between devices by JAX's collectives and lax.ppermute only.
A program may use at most 128 MiB of HBM per device.

```python
import math
import jax
import jax.numpy as jnp
from jax import lax

C = 192
HEADS = 6
HD = 32
WZ = 4
WY = 8
WX = 8
SZ = 2
SY = 4
SX = 4
WT = 256
TABLE = 1575
CZ = 4
CY = 8
CX = 16
NZ = 128
NY = 64
NX = 32
TOKENS = 262144


def draw_tokens(key, part):
    key = jax.random.fold_in(key, 11)
    first_term = jax.random.fold_in(key, 0)
    shape = (NZ, NY, NX, C)
    value_rows = jax.random.truncated_normal(first_term, -4.0, 4.0, shape, jnp.float32)
    return jnp.clip(value_rows, -4.5, 4.5).astype(jnp.bfloat16)


def draw_qkv_weight(key, part):
    key = jax.random.fold_in(key, 23)
    first_term = jax.random.fold_in(key, 0)
    value_rows = jax.random.truncated_normal(first_term, -4.0, 4.0, (C, 3 * C), jnp.float32) / jnp.sqrt(jnp.float32(C))
    return jnp.clip(value_rows, -3.0, 3.0).astype(jnp.bfloat16)


def draw_grad_out(key, part):
    key = jax.random.fold_in(key, 37)
    first_term, second_term = jax.random.split(key, 2)
    blocks = (NZ // CZ, NY // CY, NX // CX)
    scales = jnp.exp(jax.random.uniform(second_term, blocks, jnp.float32, 0.0, math.log(10.0))) / 4.6
    scales = jnp.broadcast_to(scales[:, None, :, None, :, None], (NZ // CZ, CZ, NY // CY, CY, NX // CX, CX))
    scales = scales.reshape(NZ, NY, NX, 1)
    shape = (NZ, NY, NX, C)
    value_rows = jax.random.truncated_normal(first_term, -4.0, 4.0, shape, jnp.float32)
    return jnp.clip(value_rows * scales, -9.0, 9.0).astype(jnp.bfloat16)


def centred(stream_key, dims, deviation, bound, kind=jnp.bfloat16):
    array = jax.random.normal(stream_key, dims, jnp.float32) * deviation
    return jnp.minimum(jnp.maximum(array, -bound), bound).astype(kind)


def setup_inputs(seed: int = 0) -> dict:
    streams_of = jax.random.split(jax.random.key(seed), 9)
    tokens = draw_tokens(jax.random.fold_in(streams_of[8], 71), 0)
    layer_norm_gain = jnp.clip(1.0 + 0.15 * jax.random.normal(streams_of[1], (C,), jnp.float32), 0.25, 1.75)
    layer_norm_bias = centred(streams_of[2], (C,), 0.5, 3.0, jnp.float32)
    qkv_weight = draw_qkv_weight(jax.random.fold_in(streams_of[8], 71), 0)
    qkv_bias = centred(streams_of[4], (3 * C,), 0.5, 3.0, jnp.float32)
    proj_weight = centred(streams_of[5], (C, C), C ** -0.5, 0.4375)
    bias_table = centred(streams_of[6], (HEADS, TABLE), 1.0, 4.0, jnp.float32)
    grad_out = draw_grad_out(jax.random.fold_in(streams_of[8], 71), 0)
    return {"tokens": tokens, "layer_norm_gain": layer_norm_gain, "layer_norm_bias": layer_norm_bias, "qkv_weight": qkv_weight, "qkv_bias": qkv_bias, "proj_weight": proj_weight, "bias_table": bias_table, "grad_out": grad_out}


EPSILON = 1e-05
MASKED = -100.0

def relative_index():
    position = jnp.arange(WT, dtype=jnp.int32)
    depth_pos = position // (WY * WX)
    row_pos = position // WX % WY
    col_pos = position % WX
    index = (depth_pos[:, None] - depth_pos[None, :] + WZ - 1) * ((2 * WY - 1) * (2 * WX - 1))
    index = index + (row_pos[:, None] - row_pos[None, :] + WY - 1) * (2 * WX - 1)
    index = index + (col_pos[:, None] - col_pos[None, :] + WX - 1)
    return index.astype(jnp.int32)

def windows_of(field):
    depth, rows, cols = field.shape[:3]
    rest = field.shape[3:]
    field = field.reshape((depth // WZ, WZ, rows // WY, WY, cols // WX, WX) + rest)
    order = (0, 2, 4, 1, 3, 5) + tuple(range(6, 6 + len(rest)))
    return field.transpose(order).reshape((-1, WT) + rest)

def grid_of(windows, depth, rows, cols):
    rest = windows.shape[2:]
    field = windows.reshape((depth // WZ, rows // WY, cols // WX, WZ, WY, WX) + rest)
    order = (0, 3, 1, 4, 2, 5) + tuple(range(6, 6 + len(rest)))
    return field.transpose(order).reshape((depth, rows, cols) + rest)

def apply_layer_norm(field, gain_vector, bias_vector):
    value_rows = field.astype(jnp.float32)
    centered_values = lax.optimization_barrier(jnp.mean(value_rows, -1, keepdims=True))
    spread = lax.optimization_barrier(jnp.mean((value_rows - centered_values) ** 2, -1, keepdims=True))
    reciprocal_deviation = lax.rsqrt(spread + EPSILON)
    standardized_input = (value_rows - centered_values) * reciprocal_deviation
    return ((standardized_input * gain_vector + bias_vector).astype(jnp.bfloat16), standardized_input, reciprocal_deviation)

def norm_backward_step(normed_gradient, standardized_input, reciprocal_deviation, gain_vector):
    standardized_gradient = normed_gradient * gain_vector
    first_term = lax.optimization_barrier(jnp.mean(standardized_gradient, -1, keepdims=True))
    second_term = lax.optimization_barrier(jnp.mean(standardized_gradient * standardized_input, -1, keepdims=True))
    return reciprocal_deviation * (standardized_gradient - first_term - standardized_input * second_term)

def region_of(coord, total, width, half):
    return (coord >= total - width).astype(jnp.int32) + (coord >= total - half).astype(jnp.int32)

def window_backward(normed_w, cot_w, region_w, qkv_weight, qkv_bias, proj_weight, bias_full):
    groups = normed_w.shape[0]
    factor = HD ** (-0.5)
    f32 = jnp.float32
    flat_normed = normed_w.reshape(-1, C)
    qkv = (jnp.dot(flat_normed, qkv_weight, preferred_element_type=f32) + qkv_bias).astype(jnp.bfloat16)
    qkv = qkv.reshape(groups, WT, 3, HEADS, HD).transpose(2, 0, 3, 1, 4)
    query, keys_all, value_rows = (qkv[0], qkv[1], qkv[2])
    shared = region_w[:, :, None] == region_w[:, None, :]
    penalty = jnp.where(shared, 0.0, MASKED).astype(f32)[:, None]
    scores = jnp.einsum('ghqd,ghkd->ghqk', query.astype(f32), keys_all.astype(f32)) * factor
    scores = scores + bias_full[None] + penalty
    highest = lax.optimization_barrier(jnp.max(scores, -1, keepdims=True))
    exponent = jnp.exp(scores - highest)
    probs = exponent / lax.optimization_barrier(jnp.sum(exponent, -1, keepdims=True))
    probs_b = probs.astype(jnp.bfloat16)
    attended = jnp.einsum('ghqk,ghkd->ghqd', probs_b.astype(f32), value_rows.astype(f32)).astype(jnp.bfloat16)
    attended = attended.transpose(0, 2, 1, 3).reshape(-1, C)
    flat_cot = cot_w.reshape(-1, C)
    grad_proj = lax.dot_general(attended, flat_cot, (((0,), (0,)), ((), ())), preferred_element_type=f32)
    d_att = jnp.dot(flat_cot, proj_weight.T, preferred_element_type=f32).astype(jnp.bfloat16)
    d_att = d_att.reshape(groups, WT, HEADS, HD).transpose(0, 2, 1, 3)
    d_probs = jnp.einsum('ghqd,ghkd->ghqk', d_att.astype(f32), value_rows.astype(f32))
    d_values = jnp.einsum('ghqk,ghqd->ghkd', probs_b.astype(f32), d_att.astype(f32)).astype(jnp.bfloat16)
    d_scores = probs * (d_probs - lax.optimization_barrier(jnp.sum(probs * d_probs, -1, keepdims=True)))
    d_scores_b = d_scores.astype(jnp.bfloat16)
    d_query = (jnp.einsum('ghqk,ghkd->ghqd', d_scores_b.astype(f32), keys_all.astype(f32)) * factor).astype(jnp.bfloat16)
    d_keys = (jnp.einsum('ghqk,ghqd->ghkd', d_scores_b.astype(f32), query.astype(f32)) * factor).astype(jnp.bfloat16)
    d_qkv = jnp.stack([d_query, d_keys, d_values], 0).transpose(1, 3, 0, 2, 4).reshape(-1, 3 * C)
    grad_qkv = lax.dot_general(flat_normed, d_qkv, (((0,), (0,)), ((), ())), preferred_element_type=f32)
    grad_qkv_b = lax.optimization_barrier(jnp.sum(d_qkv.astype(f32), 0))
    normed_gradient = jnp.dot(d_qkv, qkv_weight.T, preferred_element_type=f32).reshape(groups, WT, C)
    return (normed_gradient, grad_proj, grad_qkv, grad_qkv_b, lax.optimization_barrier(jnp.sum(d_scores, 0)))

def reference(tokens, layer_norm_gain, layer_norm_bias, qkv_weight, qkv_bias, proj_weight, bias_table, grad_out):
    f32 = jnp.float32
    shifted_tokens = jnp.roll(tokens, (-SZ, -SY, -SX), axis=(0, 1, 2))
    shifted_cot = jnp.roll(grad_out, (-SZ, -SY, -SX), axis=(0, 1, 2))
    index = relative_index()
    bias_full = jnp.take(bias_table, index, axis=1)
    region_z = region_of(jnp.arange(NZ, dtype=jnp.int32), NZ, WZ, SZ)
    region_y = region_of(jnp.arange(NY, dtype=jnp.int32), NY, WY, SY)
    region_x = region_of(jnp.arange(NX, dtype=jnp.int32), NX, WX, SX)
    region = region_z[:, None, None] * 9 + region_y[None, :, None] * 3 + region_x[None, None, :]
    slabs = (shifted_tokens.reshape(NZ // WZ, WZ, NY, NX, C), shifted_cot.reshape(NZ // WZ, WZ, NY, NX, C), region.reshape(NZ // WZ, WZ, NY, NX))

    def visit(carry, slab):
        token_block_rows, cot_slab, region_slab = slab
        normed_tokens, standardized_input, reciprocal_deviation = apply_layer_norm(token_block_rows, layer_norm_gain, layer_norm_bias)
        result = window_backward(windows_of(normed_tokens), windows_of(cot_slab), windows_of(region_slab), qkv_weight, qkv_bias, proj_weight, bias_full)
        normed_gradient = grid_of(result[0], WZ, NY, NX)
        shifted_gradient_rows = norm_backward_step(normed_gradient, standardized_input, reciprocal_deviation, layer_norm_gain)
        shifted_grad = (cot_slab.astype(f32) + shifted_gradient_rows).astype(jnp.bfloat16)
        gain_product = lax.optimization_barrier(jnp.sum(normed_gradient * standardized_input, (0, 1, 2)))
        shift_term = lax.optimization_barrier(jnp.sum(normed_gradient, (0, 1, 2)))
        terms = (result[1], result[2], result[3], result[4], gain_product, shift_term)
        return (tuple((a + b for a, b in zip(carry, terms))), shifted_grad)
    init = (jnp.zeros((C, C), f32), jnp.zeros((C, 3 * C), f32), jnp.zeros((3 * C,), f32), jnp.zeros((HEADS, WT, WT), f32), jnp.zeros((C,), f32), jnp.zeros((C,), f32))
    sums, grads = lax.scan(visit, init, slabs)
    shifted_grad = grads.reshape(NZ, NY, NX, C)
    grad_tokens = jnp.roll(shifted_grad, (SZ, SY, SX), axis=(0, 1, 2))
    table_sum = jax.ops.segment_sum(sums[3].reshape(HEADS, -1).T, index.reshape(-1), num_segments=TABLE).T
    factor = 1.0 / math.sqrt(TOKENS)
    return (grad_tokens, sums[4] * factor, sums[5] * factor, sums[1] * factor, sums[2] * factor, sums[0] * factor, table_sum * factor)
```

```python
import functools
import math

import jax
import jax.numpy as jnp
import numpy as np
from jax import lax
from jax.experimental import pallas as pl
from jax.experimental.pallas import tpu as pltpu
from jax.sharding import Mesh
from jax.sharding import PartitionSpec as P

C = 192
HEADS = 6
HD = 32
WZ, WY, WX = 4, 8, 8
SZ, SY, SX = 2, 4, 4
WT = 256
TABLE = 1575
EPSILON = 1e-05
MASKED = -100.0
FACTOR = HD ** (-0.5)
GZ = ("yh", "z")
AXES = ("yh", "z", "gy", "gx")
ROWS = 1280
TABLE_ROWS = 6 * C
F32 = jnp.float32
BF16 = jnp.bfloat16


def nn(a, b):
    return lax.dot_general(a, b, (((1,), (0,)), ((), ())), preferred_element_type=F32)


def nt(a, b):
    return lax.dot_general(a, b, (((1,), (1,)), ((), ())), preferred_element_type=F32)


def shifted(value, axis, steps):
    count = lax.axis_size(axis)
    pairs = [(source, (source + steps) % count) for source in range(count)]
    return lax.ppermute(value, axis, pairs)


def roll_lanes(value, steps):
    steps %= WT
    return value if steps == 0 else pltpu.roll(value, steps, 1)


def roll_rows_forward(value):
    return pltpu.roll(value, 0, 1, stride=1, stride_axis=0)


def iota(shape, dim):
    return lax.broadcasted_iota(jnp.int32, shape, dim)


def expand_bias(classes, lane):
    row = iota((8, WT), 0)
    z_slot, y_slot, x_slot = lane // 64, lane // 8 % 8, lane % 8
    by_x = {}
    for sz in range(2):
        for sy in range(2):
            at = sz * 4 + sy * 2
            below = jnp.broadcast_to(roll_lanes(classes[at : at + 1], -8), (8, WT))
            above = jnp.broadcast_to(classes[at + 1 : at + 2], (8, WT))
            by_x[sz, sy] = jnp.where(
                x_slot >= row, roll_rows_forward(above), roll_rows_forward(below)
            )
    parts = []
    for zk in range(WZ):
        by_z = [
            roll_lanes(jnp.where(z_slot < WZ - zk, by_x[1, sy], by_x[0, sy]), 64 * zk)
            for sy in range(2)
        ]
        below = roll_lanes(by_z[0], -64)
        for yk in range(WY):
            parts.append(roll_lanes(jnp.where(y_slot < WY - yk, by_z[1], below), 8 * yk))
    return jnp.concatenate(parts, 0)


def collect_bias(pair_sums, lane):
    row = iota((8, WT), 0)
    z_slot, y_slot, x_slot = lane // 64, lane // 8 % 8, lane % 8
    by_z = [[None, None], [None, None]]
    for zk in range(WZ):
        above = below = None
        for yk in range(WY):
            at = (zk * WY + yk) * WX
            part = roll_lanes(pair_sums[at : at + 8], -8 * yk)
            stays = y_slot < WY - yk
            up = jnp.where(stays, part, 0.0)
            above = up if above is None else above + up
            if yk:
                down = jnp.where(stays, 0.0, part)
                below = down if below is None else below + down
        below = roll_lanes(below, 64)
        stays = z_slot < WZ - zk
        for sy, value in enumerate((below, above)):
            value = roll_lanes(value, -64 * zk)
            for sz, term in enumerate((jnp.where(stays, 0.0, value), jnp.where(stays, value, 0.0))):
                old = by_z[sz][sy]
                by_z[sz][sy] = term if old is None else old + term
    out = []
    for sz in range(2):
        for sy in range(2):
            value = by_z[sz][sy]
            turned = value
            for xk in range(1, WX):
                turned = jnp.where(row == xk, roll_lanes(value, -xk), turned)
            stays = x_slot < WX - row
            out.append(roll_lanes(jnp.sum(jnp.where(stays, 0.0, turned), 0, keepdims=True), 8))
            out.append(jnp.sum(jnp.where(stays, turned, 0.0), 0, keepdims=True))
    return jnp.concatenate(out, 0)


def quadrants(own, y_part, z_part, zy_part, at):
    near, far = (
        jnp.concatenate([ref[:, :, at : at + 8, :].astype(F32) for ref in pair], 1)
        for pair in ((own, y_part), (z_part, zy_part))
    )
    return jnp.concatenate([near, far], 0).reshape(WT, C)


def kernel(
    scale,
    flags_ref,
    own_ref,
    y_ref,
    z_ref,
    zy_ref,
    gain_ref,
    beta_ref,
    w_ref,
    wt_ref,
    qkv_bias_ref,
    qkv_bias_t_ref,
    proj_ref,
    table_ref,
    own_grad_ref,
    y_grad_ref,
    z_grad_ref,
    zy_grad_ref,
    sums_ref,
    xhat_s,
    rstd_s,
    normed_s,
    cot_s,
    qkv_s,
    qkvt_s,
    datt_s,
    dattt_s,
    attt_s,
    dqt_s,
    dkv_s,
    pen_s,
    table_s,
):
    gain = gain_ref[...]
    beta = beta_ref[...]
    lane = iota((8, WT), 1)
    lane_row = iota((1, WT), 1)
    sub_col = iota((WT, 1), 0)

    for w in range(2):
        parts = (own_ref, y_ref, z_ref, zy_ref)
        tok = quadrants(*(ref.at[0] for ref in parts), 8 * w)
        cot = quadrants(*(ref.at[1] for ref in parts), 8 * w).astype(BF16)
        mean = jnp.mean(tok, -1, keepdims=True)
        centred = tok - mean
        rstd = lax.rsqrt(jnp.mean(centred * centred, -1, keepdims=True) + EPSILON)
        xhat = centred * rstd
        normed = (xhat * gain + beta).astype(BF16)
        xhat_s[w] = xhat
        rstd_s[w] = rstd
        normed_s[w] = normed
        cot_s[w] = cot
        for p in range(3):
            qkv_s[w, p] = (nn(normed, w_ref[p]) + qkv_bias_ref[p]).astype(BF16)
            qkvt_s[w, p] = (nt(wt_ref[p], normed) + qkv_bias_t_ref[p]).astype(BF16)
        datt_s[w] = nt(cot, proj_ref[...]).astype(BF16)
        dattt_s[w] = nt(proj_ref[...], cot).astype(BF16)

        fz, fy = flags_ref[0], flags_ref[1]
        fx = flags_ref[2] if w else 0

        def code(t):
            half = (t // 128) * fz * 4 + (t // 32 % 2) * fy * 2
            return half + (t // 4 % 2) * fx if w else half

        pen_s[w] = jnp.where(code(sub_col) == code(lane_row), 0.0, MASKED).astype(F32)

    for h in range(HEADS):
        bias = expand_bias(table_ref[h], lane)
        pair_sums = None
        part = slice(HD * h, HD * h + HD)
        for w in range(2):
            query, keys, values = (qkv_s[w, p, :, part] for p in range(3))
            query_t, keys_t, values_t = (qkvt_s[w, p, part, :] for p in range(3))
            d_att = datt_s[w, :, part]
            d_att_t = dattt_s[w, part, :]
            scores = nn(keys, query_t) * FACTOR + bias + pen_s[w]
            exponent = jnp.exp(scores - jnp.max(scores, 0, keepdims=True))
            probs = exponent * (1.0 / jnp.sum(exponent, 0, keepdims=True))
            probs_b = probs.astype(BF16)
            attt_s[w, part, :] = nn(values_t, probs_b).astype(BF16)
            d_probs = nn(values, d_att_t)
            dkv_s[w, 1, :, part] = nn(probs_b, d_att).astype(BF16)
            d_scores = probs * (d_probs - jnp.sum(probs * d_probs, 0, keepdims=True))
            d_scores_b = d_scores.astype(BF16)
            dqt_s[w, part, :] = nn(keys_t, d_scores_b) * FACTOR
            dkv_s[w, 0, :, part] = (nn(d_scores_b, query) * FACTOR).astype(BF16)
            pair_sums = d_scores if pair_sums is None else pair_sums + d_scores
        found = collect_bias(pair_sums, lane)
        for c in range(8):
            table_s[c, h : h + 1, :] = found[c : c + 1]

    totals = [None] * 4
    vectors = [None] * 5

    def add(store, at, term):
        store[at] = term if store[at] is None else store[at] + term

    for w in range(2):
        normed = normed_s[w]
        normed_t = normed.astype(F32).T.astype(BF16)
        cot = cot_s[w]
        d_query = dqt_s[w].T.astype(BF16)
        d_normed = None
        for p, d_part in enumerate((d_query, dkv_s[w, 0], dkv_s[w, 1])):
            add(totals, p, nn(normed_t, d_part))
            add(vectors, p, jnp.sum(d_part.astype(F32), 0, keepdims=True))
            term = nn(d_part, wt_ref[p])
            d_normed = term if d_normed is None else d_normed + term
        add(totals, 3, nn(attt_s[w], cot))
        xhat = xhat_s[w]
        add(vectors, 3, jnp.sum(d_normed * xhat, 0, keepdims=True))
        add(vectors, 4, jnp.sum(d_normed, 0, keepdims=True))
        d_xhat = d_normed * gain
        first = jnp.mean(d_xhat, -1, keepdims=True)
        second = jnp.mean(d_xhat * xhat, -1, keepdims=True)
        grad = cot.astype(F32) + rstd_s[w] * (d_xhat - first - xhat * second)
        grad = grad.reshape(WZ, WY, 8, C).astype(BF16)
        cols = slice(8 * w, 8 * w + 8)
        own_grad_ref[:, :, cols, :] = grad[:SZ, :SY]
        y_grad_ref[:, :, cols, :] = grad[:SZ, SY:]
        z_grad_ref[:, :, cols, :] = grad[SZ:, :SY]
        zy_grad_ref[:, :, cols, :] = grad[SZ:, SY:]

    for p in range(4):
        sums_ref[C * p : C * p + C, :] = totals[p][:, :128] * scale
    for p in range(2):
        rest = [totals[2 * p][:, 128:], totals[2 * p + 1][:, 128:]]
        sums_ref[C * (4 + p) : C * (5 + p), :] = jnp.concatenate(rest, 1) * scale
    for c in range(8):
        table_s[c, 6:, :] = jnp.zeros((2, WT), F32)
        if c < 5:
            table_s[c, 6:7, :C] = vectors[c]
        sums_ref[TABLE_ROWS + 16 * c : TABLE_ROWS + 16 * c + 8, :] = table_s[c, :, :128] * scale
        sums_ref[TABLE_ROWS + 16 * c + 8 : TABLE_ROWS + 16 * c + 16, :] = table_s[c, :, 128:] * scale


def finish_kernel(sums_ref, qkv_ref, proj_ref, vectors_ref, table_ref):
    firsts = [sums_ref[C * p : C * p + C, :] for p in range(4)]
    rests = [sums_ref[C * (4 + p) : C * (5 + p), :] for p in range(2)]
    parts = []
    for p in range(4):
        rest = rests[p // 2]
        parts += [firsts[p], rest[:, :64] if p % 2 == 0 else rest[:, 64:]]
    qkv_ref[...] = jnp.concatenate(parts[:6], 1)
    proj_ref[...] = jnp.concatenate(parts[6:], 1)
    classes = []
    for c in range(8):
        at = TABLE_ROWS + 16 * c
        classes.append(jnp.concatenate([sums_ref[at : at + 8, :], sums_ref[at + 8 : at + 16, :]], 1))
    for c in range(5):
        vectors_ref[c : c + 1, :] = classes[c][6:7, :C]
    block = iota((8, WT), 1) // 64
    rows = []
    for index in range(1, 2 * WZ):
        sz, z = index // WZ, index % WZ
        joined = None
        for j in range(4):
            term = roll_lanes(classes[4 * sz + j], 64 * (j - z))
            joined = term if joined is None else jnp.where(block == j, term, joined)
        rows.append(joined)
    source = iota((WT, WT), 0)
    dy = source // 8 % 8 + (source // 128) * 8 - 8
    dx = source % 8 + (source // 64 % 2) * 8 - 8
    target = jnp.where((dy > -8) & (dx > -8), (dy + 7) * 15 + dx + 7, -1)
    pick = (target == iota((WT, WT), 1)).astype(F32)
    placed = lax.dot_general(
        jnp.concatenate(rows, 0),
        pick,
        (((1,), (0,)), ((), ())),
        precision=lax.Precision.HIGHEST,
        preferred_element_type=F32,
    )
    table_ref[...] = jnp.concatenate(
        [placed[8 * d : 8 * d + HEADS, :225] for d in range(2 * WZ - 1)], 1
    )


def finish(sums):
    vmem = pl.BlockSpec(memory_space=pltpu.VMEM)
    return pl.pallas_call(
        finish_kernel,
        out_shape=(
            jax.ShapeDtypeStruct((C, 3 * C), F32),
            jax.ShapeDtypeStruct((C, C), F32),
            jax.ShapeDtypeStruct((5, C), F32),
            jax.ShapeDtypeStruct((HEADS, TABLE), F32),
        ),
        in_specs=[vmem],
        out_specs=(vmem,) * 4,
        compiler_params=pltpu.CompilerParams(vmem_limit_bytes=16 * 1024 * 1024),
        name="finish",
    )(sums)


def windows(scale, *operands):
    vmem = pl.BlockSpec(memory_space=pltpu.VMEM)
    quarter = jax.ShapeDtypeStruct((SZ, SY, 16, C), BF16)
    return pl.pallas_call(
        functools.partial(kernel, scale),
        out_shape=(quarter,) * 4 + (jax.ShapeDtypeStruct((ROWS, 128), F32),),
        in_specs=[pl.BlockSpec(memory_space=pltpu.SMEM)] + [vmem] * (len(operands) - 1),
        out_specs=(vmem,) * 5,
        scratch_shapes=[
            pltpu.VMEM((2, WT, C), F32),
            pltpu.VMEM((2, WT, 1), F32),
            pltpu.VMEM((2, WT, C), BF16),
            pltpu.VMEM((2, WT, C), BF16),
            pltpu.VMEM((2, 3, WT, C), BF16),
            pltpu.VMEM((2, 3, C, WT), BF16),
            pltpu.VMEM((2, WT, C), BF16),
            pltpu.VMEM((2, C, WT), BF16),
            pltpu.VMEM((2, C, WT), BF16),
            pltpu.VMEM((2, C, WT), F32),
            pltpu.VMEM((2, 2, WT, C), BF16),
            pltpu.VMEM((2, WT, WT), F32),
            pltpu.VMEM((8, 8, WT), F32),
        ],
        compiler_params=pltpu.CompilerParams(vmem_limit_bytes=48 * 1024 * 1024),
        cost_estimate=pl.CostEstimate(
            flops=1_000_000_000, bytes_accessed=3_000_000, transcendentals=800_000
        ),
        name="windows",
    )(*operands)


def sent(value, gz=0, gy=0, gx=0):
    axes, sizes, steps = [], [], []
    for names, step in ((GZ, gz), (("gy",), gy), (("gx",), gx)):
        if step:
            axes += names
            sizes.append(math.prod(lax.axis_size(a) for a in names))
            steps.append(step)
    pairs = []
    for place in np.ndindex(*sizes):
        to = tuple((p + s) % n for p, s, n in zip(place, steps, sizes))
        pairs.append(tuple(int(np.ravel_multi_index(q, sizes)) for q in (place, to)))
    return lax.ppermute(value, tuple(axes), pairs)


def shift_pair(stacked):
    border = sent(stacked[:, :, :, :SX], gx=-1)
    stacked = jnp.concatenate([stacked[:, :, :, SX:], border], 3)
    y_part = sent(stacked[:, SZ:, :SY], gy=-1)
    z_part = sent(stacked[:, :SZ, SY:], gz=-1)
    zy_part = sent(stacked[:, :SZ, :SY], gz=-1, gy=-1)
    return stacked[:, SZ:, SY:], y_part, z_part, zy_part


def unshift_quarters(own, y_part, z_part, zy_part):
    y_part = sent(y_part, gy=1)
    z_part = sent(z_part, gz=1)
    zy_part = sent(zy_part, gz=1, gy=1)
    near = jnp.concatenate([zy_part, z_part], 1)
    far = jnp.concatenate([y_part, own], 1)
    field = jnp.concatenate([near, far], 0)
    border = sent(field[:, :, -SX:], gx=1)
    return jnp.concatenate([border, field[:, :, :-SX]], 2)


def classes_of(bias_table):
    table = bias_table.reshape(HEADS, 2 * WZ - 1, 2 * WY - 1, 2 * WX - 1)
    table = jnp.pad(table, ((0, 0), (1, 0), (1, 0), (1, 0)))
    table = table.reshape(HEADS, 2, WZ, 2, WY, 2, WX)
    return table.transpose(0, 1, 3, 5, 2, 4, 6).reshape(HEADS, 8, WT)


def swapped(value, axis, partners):
    return lax.ppermute(value, axis, list(enumerate(partners)))


def to_each(value, axis):
    count = lax.axis_size(axis)
    spread = jnp.broadcast_to(value[None], (count,) + value.shape)
    return lax.all_to_all(spread, axis, 0, 0, tiled=True)


def reduce_sums(sums):
    half = ROWS // 2
    core = lax.axis_index("gx")
    mine = lax.dynamic_slice_in_dim(sums, core * half, half, 0)
    other = lax.dynamic_slice_in_dim(sums, (1 - core) * half, half, 0)
    mine = mine + swapped(other, "gx", (1, 0))
    count = lax.axis_size("gy")
    part = lax.all_to_all(mine.reshape(count, half // count, 128), "gy", 0, 0, tiled=True).sum(0)
    part = part + swapped(part, "yh", (1, 0, 3, 2))
    part = part + swapped(part, "yh", (3, 2, 1, 0))
    part = to_each(part, "z").sum(0)
    mine = to_each(part, "gy").reshape(half, 128)
    return lax.all_gather(mine, "gx", axis=0, tiled=True)


def per_device(tokens, ln_gain, ln_bias, qkv_weight, qkv_bias, proj_weight, bias_table, grad_out):
    count = tokens.shape[0] * tokens.shape[1] * tokens.shape[2]
    for axis in AXES:
        count *= lax.axis_size(axis)
    quarters = shift_pair(jnp.stack([tokens, grad_out], 0))
    w3 = qkv_weight.reshape(C, 3, C).transpose(1, 0, 2)
    w3t = qkv_weight.T.reshape(3, C, C)
    last = [lax.axis_index(a) == lax.axis_size(a) - 1 for a in AXES]
    flags = jnp.stack([last[0] & last[1], last[2], last[3]]).astype(jnp.int32)
    *grads, sums = windows(
        1.0 / math.sqrt(count),
        flags,
        *quarters,
        ln_gain.reshape(1, C),
        ln_bias.reshape(1, C),
        w3,
        w3t,
        qkv_bias.reshape(3, 1, C),
        qkv_bias.reshape(3, C, 1),
        proj_weight,
        classes_of(bias_table),
    )
    grad_tokens = unshift_quarters(*grads)
    grad_qkv, grad_proj, vectors, grad_table = finish(reduce_sums(sums))
    return (
        grad_tokens,
        vectors[3],
        vectors[4],
        grad_qkv,
        vectors[:3].reshape(3 * C),
        grad_proj,
        grad_table,
    )


def solution(mesh):
    sizes = mesh.devices.shape
    mesh = Mesh(mesh.devices.reshape(4, sizes[0] // 4, *sizes[1:]), AXES)
    grid = P(GZ, "gy", "gx", None)
    return jax.shard_map(
        per_device,
        mesh=mesh,
        in_specs=(grid, P(), P(), P(), P(), P(), P(), grid),
        out_specs=(grid, P(), P(), P(), P(), P(), P()),
        check_vma=False,
    )
```

```python
import functools
import math

import jax
import jax.numpy as jnp
import numpy as np
from jax import lax
from jax.experimental import pallas as pl
from jax.experimental.pallas import tpu as pltpu
from jax.sharding import Mesh
from jax.sharding import PartitionSpec as P

C = 192
HEADS = 6
HD = 32
WZ, WY, WX = 4, 8, 8
SZ, SY, SX = 2, 4, 4
WT = 256
TABLE = 1575
EPSILON = 1e-05
MASKED = -100.0
FACTOR = HD ** (-0.5)
GZ = ("yh", "z")
PLANE = ("yh", "gy")
AXES = ("yh", "z", "gy", "gx")
ROWS = 1536
TABLE_ROWS = 6 * C
USED = TABLE_ROWS + 128
F32 = jnp.float32
BF16 = jnp.bfloat16


def nn(a, b):
    return lax.dot_general(a, b, (((1,), (0,)), ((), ())), preferred_element_type=F32)


def nt(a, b):
    return lax.dot_general(a, b, (((1,), (1,)), ((), ())), preferred_element_type=F32)


def shifted(value, axis, steps):
    count = lax.axis_size(axis)
    pairs = [(source, (source + steps) % count) for source in range(count)]
    return lax.ppermute(value, axis, pairs)


def roll_lanes(value, steps):
    steps %= WT
    return value if steps == 0 else pltpu.roll(value, steps, 1)


def roll_rows_forward(value):
    return pltpu.roll(value, 0, 1, stride=1, stride_axis=0)


def iota(shape, dim):
    return lax.broadcasted_iota(jnp.int32, shape, dim)


def expand_bias(classes, lane):
    row = iota((8, WT), 0)
    z_slot, y_slot, x_slot = lane // 64, lane // 8 % 8, lane % 8
    by_x = {}
    for sz in range(2):
        for sy in range(2):
            at = sz * 4 + sy * 2
            below = jnp.broadcast_to(roll_lanes(classes[at : at + 1], -8), (8, WT))
            above = jnp.broadcast_to(classes[at + 1 : at + 2], (8, WT))
            by_x[sz, sy] = jnp.where(
                x_slot >= row, roll_rows_forward(above), roll_rows_forward(below)
            )
    parts = []
    for zk in range(WZ):
        by_z = [
            roll_lanes(jnp.where(z_slot < WZ - zk, by_x[1, sy], by_x[0, sy]), 64 * zk)
            for sy in range(2)
        ]
        below = roll_lanes(by_z[0], -64)
        for yk in range(WY):
            parts.append(roll_lanes(jnp.where(y_slot < WY - yk, by_z[1], below), 8 * yk))
    return jnp.concatenate(parts, 0)


def collect_bias(pair_sums, lane):
    row = iota((8, WT), 0)
    z_slot, y_slot, x_slot = lane // 64, lane // 8 % 8, lane % 8
    by_z = [[None, None], [None, None]]
    for zk in range(WZ):
        above = below = None
        for yk in range(WY):
            at = (zk * WY + yk) * WX
            part = roll_lanes(pair_sums[at : at + 8], -8 * yk)
            stays = y_slot < WY - yk
            up = jnp.where(stays, part, 0.0)
            above = up if above is None else above + up
            if yk:
                down = jnp.where(stays, 0.0, part)
                below = down if below is None else below + down
        below = roll_lanes(below, 64)
        stays = z_slot < WZ - zk
        for sy, value in enumerate((below, above)):
            value = roll_lanes(value, -64 * zk)
            for sz, term in enumerate((jnp.where(stays, 0.0, value), jnp.where(stays, value, 0.0))):
                old = by_z[sz][sy]
                by_z[sz][sy] = term if old is None else old + term
    out = []
    for sz in range(2):
        for sy in range(2):
            value = by_z[sz][sy]
            turned = value
            for xk in range(1, WX):
                turned = jnp.where(row == xk, roll_lanes(value, -xk), turned)
            stays = x_slot < WX - row
            out.append(roll_lanes(jnp.sum(jnp.where(stays, 0.0, turned), 0, keepdims=True), 8))
            out.append(jnp.sum(jnp.where(stays, turned, 0.0), 0, keepdims=True))
    return jnp.concatenate(out, 0)


def block_of(own, y_part, z_part, zy_part):
    near, far = (
        jnp.concatenate([ref[...].astype(F32) for ref in pair], 1)
        for pair in ((own, y_part), (z_part, zy_part))
    )
    return jnp.concatenate([near, far], 0).reshape(WZ * WY, 16, 2 * C)


def windows_of(block, border):
    first, second = block[:, :8], block[:, 8:]
    border = jnp.concatenate([border, border], 1)
    early = iota((WZ * WY, 8, 2 * C), 1) < SX
    return [
        pltpu.roll(jnp.where(early, right, left), SX, 1).reshape(WT, 2 * C)
        for left, right in ((first, second), (second, border))
    ]


def columns_of(windows):
    early = iota((WZ * WY, 8, C), 1) < SX
    first, second = (pltpu.roll(w.reshape(WZ * WY, 8, C), SX, 1) for w in windows)
    block = jnp.concatenate([first, jnp.where(early, first, second)], 1)
    return block.reshape(WZ, WY, 16, C), second.reshape(WZ, WY, 8, C)


def kernel(
    scale,
    flags_ref,
    z_ref,
    zy_ref,
    y_ref,
    own_ref,
    border_ref,
    norm_ref,
    w_ref,
    wt_ref,
    qkv_bias_ref,
    qkv_bias_t_ref,
    proj_ref,
    table_ref,
    grad_ref,
    border_grad_ref,
    sums_ref,
    xhat_s,
    rstd_s,
    normed_s,
    cot_s,
    qkv_s,
    qkvt_s,
    datt_s,
    dattt_s,
    attt_s,
    dqt_s,
    dkv_s,
    pen_s,
    table_s,
):
    gain = norm_ref[0:1, :]
    beta = norm_ref[1:2, :]
    lane = iota((8, WT), 1)
    lane_row = iota((1, WT), 1)
    sub_col = iota((WT, 1), 0)

    block = block_of(own_ref, y_ref, z_ref, zy_ref)
    border = jnp.concatenate([border_ref[SZ:], border_ref[:SZ]], 0).astype(F32)
    both = windows_of(block, border.reshape(WZ * WY, SX, 2 * C))
    for w in range(2):
        tok = both[w][:, :C]
        cot = both[w][:, C:].astype(BF16)
        mean = jnp.mean(tok, -1, keepdims=True)
        centred = tok - mean
        rstd = lax.rsqrt(jnp.mean(centred * centred, -1, keepdims=True) + EPSILON)
        xhat = centred * rstd
        normed = (xhat * gain + beta).astype(BF16)
        xhat_s[w] = xhat
        rstd_s[w] = rstd
        normed_s[w] = normed
        cot_s[w] = cot
        for p in range(3):
            qkv_s[w, p] = (nn(normed, w_ref[p]) + qkv_bias_ref[p]).astype(BF16)
            qkvt_s[w, p] = (nt(wt_ref[p], normed) + qkv_bias_t_ref[p]).astype(BF16)
        datt_s[w] = nt(cot, proj_ref[...]).astype(BF16)
        dattt_s[w] = nt(proj_ref[...], cot).astype(BF16)

        fz, fy = flags_ref[0], flags_ref[1]
        fx = flags_ref[2] if w else 0

        def code(t):
            half = (t // 128) * fz * 4 + (t // 32 % 2) * fy * 2
            return half + (t // 4 % 2) * fx if w else half

        pen_s[w] = jnp.where(code(sub_col) == code(lane_row), 0.0, MASKED).astype(F32)

    for h in range(HEADS):
        bias = expand_bias(table_ref[h], lane)
        pair_sums = None
        part = slice(HD * h, HD * h + HD)
        for w in range(2):
            query, keys, values = (qkv_s[w, p, :, part] for p in range(3))
            query_t, keys_t, values_t = (qkvt_s[w, p, part, :] for p in range(3))
            d_att = datt_s[w, :, part]
            d_att_t = dattt_s[w, part, :]
            scores = nn(keys, query_t) * FACTOR + bias + pen_s[w]
            exponent = jnp.exp(scores - jnp.max(scores, 0, keepdims=True))
            probs = exponent * (1.0 / jnp.sum(exponent, 0, keepdims=True))
            probs_b = probs.astype(BF16)
            attt_s[w, part, :] = nn(values_t, probs_b).astype(BF16)
            d_probs = nn(values, d_att_t)
            dkv_s[w, 1, :, part] = nn(probs_b, d_att).astype(BF16)
            d_scores = probs * (d_probs - jnp.sum(probs * d_probs, 0, keepdims=True))
            d_scores_b = d_scores.astype(BF16)
            dqt_s[w, part, :] = nn(keys_t, d_scores_b) * FACTOR
            dkv_s[w, 0, :, part] = (nn(d_scores_b, query) * FACTOR).astype(BF16)
            pair_sums = d_scores if pair_sums is None else pair_sums + d_scores
        found = collect_bias(pair_sums, lane)
        for c in range(8):
            table_s[c, h : h + 1, :] = found[c : c + 1]

    totals = [None] * 4
    vectors = [None] * 5
    grads = []

    def add(store, at, term):
        store[at] = term if store[at] is None else store[at] + term

    for w in range(2):
        normed = normed_s[w]
        normed_t = normed.astype(F32).T.astype(BF16)
        cot = cot_s[w]
        d_query = dqt_s[w].T.astype(BF16)
        d_normed = None
        for p, d_part in enumerate((d_query, dkv_s[w, 0], dkv_s[w, 1])):
            add(totals, p, nn(normed_t, d_part))
            add(vectors, p, jnp.sum(d_part.astype(F32), 0, keepdims=True))
            term = nn(d_part, wt_ref[p])
            d_normed = term if d_normed is None else d_normed + term
        add(totals, 3, nn(attt_s[w], cot))
        xhat = xhat_s[w]
        add(vectors, 3, jnp.sum(d_normed * xhat, 0, keepdims=True))
        add(vectors, 4, jnp.sum(d_normed, 0, keepdims=True))
        d_xhat = d_normed * gain
        first = jnp.mean(d_xhat, -1, keepdims=True)
        second = jnp.mean(d_xhat * xhat, -1, keepdims=True)
        grad = cot.astype(F32) + rstd_s[w] * (d_xhat - first - xhat * second)
        grads.append(grad)

    block, border = columns_of(grads)
    grad_ref[...] = block.astype(BF16)
    border_grad_ref[...] = border.astype(BF16)
    for p in range(4):
        sums_ref[C * p : C * p + C, :] = totals[p][:, :128] * scale
    for p in range(2):
        rest = [totals[2 * p][:, 128:], totals[2 * p + 1][:, 128:]]
        sums_ref[C * (4 + p) : C * (5 + p), :] = jnp.concatenate(rest, 1) * scale
    for c in range(8):
        table_s[c, 6:, :] = jnp.zeros((2, WT), F32)
        if c < 5:
            table_s[c, 6:7, :C] = vectors[c]
        sums_ref[TABLE_ROWS + 16 * c : TABLE_ROWS + 16 * c + 8, :] = table_s[c, :, :128] * scale
        sums_ref[TABLE_ROWS + 16 * c + 8 : TABLE_ROWS + 16 * c + 16, :] = table_s[c, :, 128:] * scale
    sums_ref[USED:, :] = jnp.zeros((ROWS - USED, 128), F32)


def finish_kernel(sums_ref, gain_ref, shift_ref, qkv_ref, bias_ref, proj_ref, table_ref):
    firsts = [sums_ref[C * p : C * p + C, :].astype(F32) for p in range(4)]
    rests = [sums_ref[C * (4 + p) : C * (5 + p), :].astype(F32) for p in range(2)]
    parts = []
    for p in range(4):
        rest = rests[p // 2]
        parts += [firsts[p], rest[:, :64] if p % 2 == 0 else rest[:, 64:]]
    qkv_ref[...] = jnp.concatenate(parts[:6], 1)
    proj_ref[...] = jnp.concatenate(parts[6:], 1)
    classes = []
    for c in range(8):
        at = TABLE_ROWS + 16 * c
        pair = sums_ref[at : at + 16, :].astype(F32)
        classes.append(jnp.concatenate([pair[:8], pair[8:]], 1))
    vectors = [classes[c][6:7, :C] for c in range(5)]
    bias_ref[...] = jnp.concatenate(vectors[:3], 1)[0]
    gain_ref[...] = vectors[3][0]
    shift_ref[...] = vectors[4][0]
    block = iota((8, WT), 1) // 64
    rows = []
    for index in range(1, 2 * WZ):
        sz, z = index // WZ, index % WZ
        joined = None
        for j in range(4):
            term = roll_lanes(classes[4 * sz + j], 64 * (j - z))
            joined = term if joined is None else jnp.where(block == j, term, joined)
        rows.append(joined)
    source = iota((WT, WT), 0)
    dy = source // 8 % 8 + (source // 128) * 8 - 8
    dx = source % 8 + (source // 64 % 2) * 8 - 8
    target = jnp.where((dy > -8) & (dx > -8), (dy + 7) * 15 + dx + 7, -1)
    pick = (target == iota((WT, WT), 1)).astype(F32)
    placed = lax.dot_general(
        jnp.concatenate(rows, 0),
        pick,
        (((1,), (0,)), ((), ())),
        precision=lax.Precision.HIGHEST,
        preferred_element_type=F32,
    )
    table_ref[...] = jnp.concatenate(
        [placed[8 * d : 8 * d + HEADS, :225] for d in range(2 * WZ - 1)], 1
    )


def finish(sums):
    vmem = pl.BlockSpec(memory_space=pltpu.VMEM)
    return pl.pallas_call(
        finish_kernel,
        out_shape=tuple(
            jax.ShapeDtypeStruct(shape, F32)
            for shape in ((C,), (C,), (C, 3 * C), (3 * C,), (C, C), (HEADS, TABLE))
        ),
        in_specs=[vmem],
        out_specs=(vmem,) * 6,
        compiler_params=pltpu.CompilerParams(vmem_limit_bytes=16 * 1024 * 1024),
        name="finish",
    )(sums)


def windows(scale, *operands):
    vmem = pl.BlockSpec(memory_space=pltpu.VMEM)
    return pl.pallas_call(
        functools.partial(kernel, scale),
        out_shape=(
            jax.ShapeDtypeStruct((WZ, WY, 16, C), BF16),
            jax.ShapeDtypeStruct((WZ, WY, 8, C), BF16),
            jax.ShapeDtypeStruct((ROWS, 128), F32),
        ),
        in_specs=[pl.BlockSpec(memory_space=pltpu.SMEM)] + [vmem] * (len(operands) - 1),
        out_specs=(vmem,) * 3,
        scratch_shapes=[
            pltpu.VMEM((2, WT, C), F32),
            pltpu.VMEM((2, WT, 1), F32),
            pltpu.VMEM((2, WT, C), BF16),
            pltpu.VMEM((2, WT, C), BF16),
            pltpu.VMEM((2, 3, WT, C), BF16),
            pltpu.VMEM((2, 3, C, WT), BF16),
            pltpu.VMEM((2, WT, C), BF16),
            pltpu.VMEM((2, C, WT), BF16),
            pltpu.VMEM((2, C, WT), BF16),
            pltpu.VMEM((2, C, WT), F32),
            pltpu.VMEM((2, 2, WT, C), BF16),
            pltpu.VMEM((2, WT, WT), F32),
            pltpu.VMEM((8, 8, WT), F32),
        ],
        compiler_params=pltpu.CompilerParams(vmem_limit_bytes=48 * 1024 * 1024),
        cost_estimate=pl.CostEstimate(
            flops=1_000_000_000, bytes_accessed=3_000_000, transcendentals=800_000
        ),
        name="windows",
    )(*operands)


def sent(value, gz=0, gy=0, gx=0):
    axes, sizes, steps = [], [], []
    for names, step in ((GZ, gz), (("gy",), gy), (("gx",), gx)):
        if step:
            axes += names
            sizes.append(math.prod(lax.axis_size(a) for a in names))
            steps.append(step)
    pairs = []
    for place in np.ndindex(*sizes):
        to = tuple((p + s) % n for p, s, n in zip(place, steps, sizes))
        pairs.append(tuple(int(np.ravel_multi_index(q, sizes)) for q in (place, to)))
    return lax.ppermute(value, tuple(axes), pairs)


def shift_pair(tokens, grad_out):
    z_part = jnp.concatenate([tokens[:SZ, SY:], grad_out[:SZ, SY:]], -1)
    z_part, rest = after(z_part, (tokens, grad_out))
    both = jnp.concatenate(rest, -1)
    z_part = sent(z_part, gz=-1)
    zy_part = sent(both[:SZ, :SY], gz=-1, gy=-1)
    y_part = sent(both[SZ:, :SY], gy=-1)
    own = both[SZ:, SY:]
    far, near = (
        jnp.concatenate([v[:, :, :SX] for v in pair], 1)
        for pair in ((z_part, zy_part), (own, y_part))
    )
    border = sent(jnp.concatenate([far, near], 0), gx=-1)
    return z_part, zy_part, y_part, own, border


def classes_of(bias_table):
    table = bias_table.reshape(HEADS, 2 * WZ - 1, 2 * WY - 1, 2 * WX - 1)
    table = jnp.pad(table, ((0, 0), (1, 0), (1, 0), (1, 0)))
    table = table.reshape(HEADS, 2, WZ, 2, WY, 2, WX)
    return table.transpose(0, 1, 3, 5, 2, 4, 6).reshape(HEADS, 8, WT)


def swapped(value, axis, partners):
    return lax.ppermute(value, axis, list(enumerate(partners)))


def to_each(value, axes):
    count = lax.axis_size(axes)
    spread = jnp.broadcast_to(value[None], (count,) + value.shape)
    return lax.all_to_all(spread, axes, 0, 0, tiled=True)


def after(value, other):
    return lax.optimization_barrier((value, other))


def unshift_and_reduce(field, border, sums):
    half = ROWS // 2
    core = lax.axis_index("gx")
    mine = lax.dynamic_slice_in_dim(sums, core * half, half, 0)
    other = lax.dynamic_slice_in_dim(sums, (1 - core) * half, half, 0)
    mine = mine + swapped(other, "gx", (1, 0))
    border = sent(border, gx=1)[:, :, :SX]
    field = jnp.concatenate([border, field[:, :, SX:]], 2)
    y_border = sent(field[:, SY:], gy=1)
    count = lax.axis_size(PLANE)
    part = lax.all_to_all(mine.reshape(count, half // count, 128), PLANE, 0, 0, tiled=True).sum(0)
    part, y_border = after(part, y_border)
    field = jnp.concatenate([y_border, field[:, :SY]], 1)
    z_border = sent(field[SZ:], gz=1)
    part = to_each(part, "z").sum(0).astype(BF16)
    mine = to_each(part, PLANE).reshape(half, 128)
    outputs = finish(lax.all_gather(mine, "gx", axis=0, tiled=True))
    outputs, z_border = after(outputs, z_border)
    return jnp.concatenate([z_border, field[:SZ]], 0), *outputs


def per_device(tokens, ln_gain, ln_bias, qkv_weight, qkv_bias, proj_weight, bias_table, grad_out):
    count = tokens.shape[0] * tokens.shape[1] * tokens.shape[2]
    for axis in AXES:
        count *= lax.axis_size(axis)
    quarters = shift_pair(tokens, grad_out)
    w3 = qkv_weight.reshape(C, 3, C).transpose(1, 0, 2)
    w3t = qkv_weight.T.reshape(3, C, C)
    last = [lax.axis_index(a) == lax.axis_size(a) - 1 for a in AXES]
    flags = jnp.stack([last[0] & last[1], last[2], last[3]]).astype(jnp.int32)
    field, border, sums = windows(
        1.0 / math.sqrt(count),
        flags,
        *quarters,
        jnp.stack([ln_gain, ln_bias], 0),
        w3,
        w3t,
        qkv_bias.reshape(3, 1, C),
        qkv_bias.reshape(3, C, 1),
        proj_weight,
        classes_of(bias_table),
    )
    return unshift_and_reduce(field, border, sums)


def solution(mesh):
    sizes = mesh.devices.shape
    mesh = Mesh(mesh.devices.reshape(4, sizes[0] // 4, *sizes[1:]), AXES)
    grid = P(GZ, "gy", "gx", None)
    return jax.shard_map(
        per_device,
        mesh=mesh,
        in_specs=(grid, P(), P(), P(), P(), P(), P(), grid),
        out_specs=(grid, P(), P(), P(), P(), P(), P()),
        check_vma=False,
    )
```

```python
import functools
import math

import jax
import jax.numpy as jnp
import numpy as np
from jax import lax
from jax.experimental import pallas as pl
from jax.experimental.pallas import tpu as pltpu
from jax.sharding import Mesh
from jax.sharding import PartitionSpec as P

C = 192
HEADS = 6
HD = 32
WZ, WY, WX = 4, 8, 8
SZ, SY, SX = 2, 4, 4
WT = 256
TABLE = 1575
EPSILON = 1e-05
MASKED = -100.0
FACTOR = HD ** (-0.5)
GZ = ("yh", "z")
PLANE = ("yh", "gy")
AXES = ("yh", "z", "gy", "gx")
ROWS = 1536
TABLE_ROWS = 6 * C
USED = TABLE_ROWS + 128
F32 = jnp.float32
BF16 = jnp.bfloat16


def nn(a, b):
    return lax.dot_general(a, b, (((1,), (0,)), ((), ())), preferred_element_type=F32)


def nt(a, b):
    return lax.dot_general(a, b, (((1,), (1,)), ((), ())), preferred_element_type=F32)


def shifted(value, axis, steps):
    count = lax.axis_size(axis)
    pairs = [(source, (source + steps) % count) for source in range(count)]
    return lax.ppermute(value, axis, pairs)


def roll_lanes(value, steps):
    steps %= WT
    return value if steps == 0 else pltpu.roll(value, steps, 1)


def roll_rows_forward(value):
    return pltpu.roll(value, 0, 1, stride=1, stride_axis=0)


def iota(shape, dim):
    return lax.broadcasted_iota(jnp.int32, shape, dim)


def expand_bias(classes, lane):
    row = iota((8, WT), 0)
    z_slot, y_slot, x_slot = lane // 64, lane // 8 % 8, lane % 8
    by_x = {}
    for sz in range(2):
        for sy in range(2):
            at = sz * 4 + sy * 2
            below = jnp.broadcast_to(roll_lanes(classes[at : at + 1], -8), (8, WT))
            above = jnp.broadcast_to(classes[at + 1 : at + 2], (8, WT))
            by_x[sz, sy] = jnp.where(
                x_slot >= row, roll_rows_forward(above), roll_rows_forward(below)
            )
    parts = []
    for zk in range(WZ):
        by_z = [
            roll_lanes(jnp.where(z_slot < WZ - zk, by_x[1, sy], by_x[0, sy]), 64 * zk)
            for sy in range(2)
        ]
        below = roll_lanes(by_z[0], -64)
        for yk in range(WY):
            parts.append(roll_lanes(jnp.where(y_slot < WY - yk, by_z[1], below), 8 * yk))
    return jnp.concatenate(parts, 0)


def collect_bias(pair_sums, lane):
    row = iota((8, WT), 0)
    z_slot, y_slot, x_slot = lane // 64, lane // 8 % 8, lane % 8
    by_z = [[None, None], [None, None]]
    for zk in range(WZ):
        above = below = None
        for yk in range(WY):
            at = (zk * WY + yk) * WX
            part = roll_lanes(pair_sums[at : at + 8], -8 * yk)
            stays = y_slot < WY - yk
            up = jnp.where(stays, part, 0.0)
            above = up if above is None else above + up
            if yk:
                down = jnp.where(stays, 0.0, part)
                below = down if below is None else below + down
        below = roll_lanes(below, 64)
        stays = z_slot < WZ - zk
        for sy, value in enumerate((below, above)):
            value = roll_lanes(value, -64 * zk)
            for sz, term in enumerate((jnp.where(stays, 0.0, value), jnp.where(stays, value, 0.0))):
                old = by_z[sz][sy]
                by_z[sz][sy] = term if old is None else old + term
    out = []
    for sz in range(2):
        for sy in range(2):
            value = by_z[sz][sy]
            turned = value
            for xk in range(1, WX):
                turned = jnp.where(row == xk, roll_lanes(value, -xk), turned)
            stays = x_slot < WX - row
            out.append(roll_lanes(jnp.sum(jnp.where(stays, 0.0, turned), 0, keepdims=True), 8))
            out.append(jnp.sum(jnp.where(stays, turned, 0.0), 0, keepdims=True))
    return jnp.concatenate(out, 0)


def block_of(own, y_part, z_part, zy_part):
    near, far = (
        jnp.concatenate([ref[...].astype(F32) for ref in pair], 1)
        for pair in ((own, y_part), (z_part, zy_part))
    )
    return jnp.concatenate([near, far], 0).reshape(WZ * WY, 16, 2 * C)


def windows_of(block, border):
    first, second = block[:, :8], block[:, 8:]
    border = jnp.concatenate([border, border], 1)
    early = iota((WZ * WY, 8, 2 * C), 1) < SX
    return [
        pltpu.roll(jnp.where(early, right, left), SX, 1).reshape(WT, 2 * C)
        for left, right in ((first, second), (second, border))
    ]


def columns_of(windows):
    early = iota((WZ * WY, 8, C), 1) < SX
    first, second = (pltpu.roll(w.reshape(WZ * WY, 8, C), SX, 1) for w in windows)
    block = jnp.concatenate([first, jnp.where(early, first, second)], 1)
    return block.reshape(WZ, WY, 16, C), second.reshape(WZ, WY, 8, C)


def kernel(
    scale,
    flags_ref,
    z_ref,
    zy_ref,
    y_ref,
    own_ref,
    border_ref,
    norm_ref,
    w_ref,
    wt_ref,
    qkv_bias_ref,
    qkv_bias_t_ref,
    proj_ref,
    table_ref,
    grad_ref,
    border_grad_ref,
    sums_ref,
    xhat_s,
    rstd_s,
    normed_s,
    cot_s,
    qkv_s,
    qkvt_s,
    datt_s,
    dattt_s,
    attt_s,
    dqt_s,
    dkv_s,
    pen_s,
    table_s,
):
    gain = norm_ref[0:1, :]
    beta = norm_ref[1:2, :]
    lane = iota((8, WT), 1)
    lane_row = iota((1, WT), 1)
    sub_col = iota((WT, 1), 0)

    block = block_of(own_ref, y_ref, z_ref, zy_ref)
    border = jnp.concatenate([border_ref[SZ:], border_ref[:SZ]], 0).astype(F32)
    both = windows_of(block, border.reshape(WZ * WY, SX, 2 * C))
    for w in range(2):
        tok = both[w][:, :C]
        cot = both[w][:, C:].astype(BF16)
        mean = jnp.mean(tok, -1, keepdims=True)
        centred = tok - mean
        rstd = lax.rsqrt(jnp.mean(centred * centred, -1, keepdims=True) + EPSILON)
        xhat = centred * rstd
        normed = (xhat * gain + beta).astype(BF16)
        xhat_s[w] = xhat
        rstd_s[w] = rstd
        normed_s[w] = normed
        cot_s[w] = cot
        for p in range(3):
            qkv_s[w, p] = (nn(normed, w_ref[p]) + qkv_bias_ref[p]).astype(BF16)
            qkvt_s[w, p] = (nt(wt_ref[p], normed) + qkv_bias_t_ref[p]).astype(BF16)
        datt_s[w] = nt(cot, proj_ref[...]).astype(BF16)
        dattt_s[w] = nt(proj_ref[...], cot).astype(BF16)

        fz, fy = flags_ref[0], flags_ref[1]
        fx = flags_ref[2] if w else 0

        def code(t):
            half = (t // 128) * fz * 4 + (t // 32 % 2) * fy * 2
            return half + (t // 4 % 2) * fx if w else half

        pen_s[w] = jnp.where(code(sub_col) == code(lane_row), 0.0, MASKED).astype(F32)

    for h in range(HEADS):
        bias = expand_bias(table_ref[h], lane)
        pair_sums = None
        part = slice(HD * h, HD * h + HD)
        for w in range(2):
            query, keys, values = (qkv_s[w, p, :, part] for p in range(3))
            query_t, keys_t, values_t = (qkvt_s[w, p, part, :] for p in range(3))
            d_att = datt_s[w, :, part]
            d_att_t = dattt_s[w, part, :]
            scores = nn(keys, query_t) * FACTOR + bias + pen_s[w]
            exponent = jnp.exp(scores - jnp.max(scores, 0, keepdims=True))
            probs = exponent * (1.0 / jnp.sum(exponent, 0, keepdims=True))
            probs_b = probs.astype(BF16)
            attt_s[w, part, :] = nn(values_t, probs_b).astype(BF16)
            d_probs = nn(values, d_att_t)
            dkv_s[w, 1, :, part] = nn(probs_b, d_att).astype(BF16)
            d_scores = probs * (d_probs - jnp.sum(probs * d_probs, 0, keepdims=True))
            d_scores_b = d_scores.astype(BF16)
            dqt_s[w, part, :] = nn(keys_t, d_scores_b) * FACTOR
            dkv_s[w, 0, :, part] = (nn(d_scores_b, query) * FACTOR).astype(BF16)
            pair_sums = d_scores if pair_sums is None else pair_sums + d_scores
        found = collect_bias(pair_sums, lane)
        for c in range(8):
            table_s[c, h : h + 1, :] = found[c : c + 1]

    totals = [None] * 4
    vectors = [None] * 5
    grads = []

    def add(store, at, term):
        store[at] = term if store[at] is None else store[at] + term

    for w in range(2):
        normed = normed_s[w]
        normed_t = normed.astype(F32).T.astype(BF16)
        cot = cot_s[w]
        d_query = dqt_s[w].T.astype(BF16)
        d_normed = None
        for p, d_part in enumerate((d_query, dkv_s[w, 0], dkv_s[w, 1])):
            add(totals, p, nn(normed_t, d_part))
            add(vectors, p, jnp.sum(d_part.astype(F32), 0, keepdims=True))
            term = nn(d_part, wt_ref[p])
            d_normed = term if d_normed is None else d_normed + term
        add(totals, 3, nn(attt_s[w], cot))
        xhat = xhat_s[w]
        add(vectors, 3, jnp.sum(d_normed * xhat, 0, keepdims=True))
        add(vectors, 4, jnp.sum(d_normed, 0, keepdims=True))
        d_xhat = d_normed * gain
        first = jnp.mean(d_xhat, -1, keepdims=True)
        second = jnp.mean(d_xhat * xhat, -1, keepdims=True)
        grad = cot.astype(F32) + rstd_s[w] * (d_xhat - first - xhat * second)
        grads.append(grad)

    block, border = columns_of(grads)
    grad_ref[...] = block.astype(BF16)
    border_grad_ref[...] = border.astype(BF16)
    for p in range(4):
        sums_ref[C * p : C * p + C, :] = totals[p][:, :128] * scale
    for p in range(2):
        rest = [totals[2 * p][:, 128:], totals[2 * p + 1][:, 128:]]
        sums_ref[C * (4 + p) : C * (5 + p), :] = jnp.concatenate(rest, 1) * scale
    for c in range(8):
        table_s[c, 6:, :] = jnp.zeros((2, WT), F32)
        if c < 5:
            table_s[c, 6:7, :C] = vectors[c]
        sums_ref[TABLE_ROWS + 16 * c : TABLE_ROWS + 16 * c + 8, :] = table_s[c, :, :128] * scale
        sums_ref[TABLE_ROWS + 16 * c + 8 : TABLE_ROWS + 16 * c + 16, :] = table_s[c, :, 128:] * scale
    sums_ref[USED:, :] = jnp.zeros((ROWS - USED, 128), F32)


def finish_kernel(sums_ref, gain_ref, shift_ref, qkv_ref, bias_ref, proj_ref, table_ref):
    firsts = [sums_ref[C * p : C * p + C, :].astype(F32) for p in range(4)]
    rests = [sums_ref[C * (4 + p) : C * (5 + p), :].astype(F32) for p in range(2)]
    parts = []
    for p in range(4):
        rest = rests[p // 2]
        parts += [firsts[p], rest[:, :64] if p % 2 == 0 else rest[:, 64:]]
    qkv_ref[...] = jnp.concatenate(parts[:6], 1)
    proj_ref[...] = jnp.concatenate(parts[6:], 1)
    classes = []
    for c in range(8):
        at = TABLE_ROWS + 16 * c
        pair = sums_ref[at : at + 16, :].astype(F32)
        classes.append(jnp.concatenate([pair[:8], pair[8:]], 1))
    vectors = [classes[c][6:7, :C] for c in range(5)]
    bias_ref[...] = jnp.concatenate(vectors[:3], 1)[0]
    gain_ref[...] = vectors[3][0]
    shift_ref[...] = vectors[4][0]
    block = iota((8, WT), 1) // 64
    rows = []
    for index in range(1, 2 * WZ):
        sz, z = index // WZ, index % WZ
        joined = None
        for j in range(4):
            term = roll_lanes(classes[4 * sz + j], 64 * (j - z))
            joined = term if joined is None else jnp.where(block == j, term, joined)
        rows.append(joined)
    source = iota((WT, WT), 0)
    dy = source // 8 % 8 + (source // 128) * 8 - 8
    dx = source % 8 + (source // 64 % 2) * 8 - 8
    target = jnp.where((dy > -8) & (dx > -8), (dy + 7) * 15 + dx + 7, -1)
    pick = (target == iota((WT, WT), 1)).astype(F32)
    placed = lax.dot_general(
        jnp.concatenate(rows, 0),
        pick,
        (((1,), (0,)), ((), ())),
        precision=lax.Precision.HIGHEST,
        preferred_element_type=F32,
    )
    table_ref[...] = jnp.concatenate(
        [placed[8 * d : 8 * d + HEADS, :225] for d in range(2 * WZ - 1)], 1
    )


def finish(sums):
    vmem = pl.BlockSpec(memory_space=pltpu.VMEM)
    return pl.pallas_call(
        finish_kernel,
        out_shape=tuple(
            jax.ShapeDtypeStruct(shape, F32)
            for shape in ((C,), (C,), (C, 3 * C), (3 * C,), (C, C), (HEADS, TABLE))
        ),
        in_specs=[vmem],
        out_specs=(vmem,) * 6,
        compiler_params=pltpu.CompilerParams(vmem_limit_bytes=16 * 1024 * 1024),
        name="finish",
    )(sums)


def windows(scale, *operands):
    vmem = pl.BlockSpec(memory_space=pltpu.VMEM)
    return pl.pallas_call(
        functools.partial(kernel, scale),
        out_shape=(
            jax.ShapeDtypeStruct((WZ, WY, 16, C), BF16),
            jax.ShapeDtypeStruct((WZ, WY, 8, C), BF16),
            jax.ShapeDtypeStruct((ROWS, 128), F32),
        ),
        in_specs=[pl.BlockSpec(memory_space=pltpu.SMEM)] + [vmem] * (len(operands) - 1),
        out_specs=(vmem,) * 3,
        scratch_shapes=[
            pltpu.VMEM((2, WT, C), F32),
            pltpu.VMEM((2, WT, 1), F32),
            pltpu.VMEM((2, WT, C), BF16),
            pltpu.VMEM((2, WT, C), BF16),
            pltpu.VMEM((2, 3, WT, C), BF16),
            pltpu.VMEM((2, 3, C, WT), BF16),
            pltpu.VMEM((2, WT, C), BF16),
            pltpu.VMEM((2, C, WT), BF16),
            pltpu.VMEM((2, C, WT), BF16),
            pltpu.VMEM((2, C, WT), F32),
            pltpu.VMEM((2, 2, WT, C), BF16),
            pltpu.VMEM((2, WT, WT), F32),
            pltpu.VMEM((8, 8, WT), F32),
        ],
        compiler_params=pltpu.CompilerParams(vmem_limit_bytes=48 * 1024 * 1024),
        cost_estimate=pl.CostEstimate(
            flops=1_000_000_000, bytes_accessed=3_000_000, transcendentals=800_000
        ),
        name="windows",
    )(*operands)


def sent(value, gz=0, gy=0, gx=0):
    axes, sizes, steps = [], [], []
    for names, step in ((GZ, gz), (("gy",), gy), (("gx",), gx)):
        if step:
            axes += names
            sizes.append(math.prod(lax.axis_size(a) for a in names))
            steps.append(step)
    pairs = []
    for place in np.ndindex(*sizes):
        to = tuple((p + s) % n for p, s, n in zip(place, steps, sizes))
        pairs.append(tuple(int(np.ravel_multi_index(q, sizes)) for q in (place, to)))
    return lax.ppermute(value, tuple(axes), pairs)


def shift_pair(tokens, grad_out):
    both = jnp.concatenate([tokens, grad_out], -1)
    z_part = sent(both[:SZ, SY:], gz=-1)
    zy_part = sent(both[:SZ, :SY], gz=-1, gy=-1)
    y_part = sent(both[SZ:, :SY], gy=-1)
    own = both[SZ:, SY:]
    far, near = (
        jnp.concatenate([v[:, :, :SX] for v in pair], 1)
        for pair in ((z_part, zy_part), (own, y_part))
    )
    border = sent(jnp.concatenate([far, near], 0), gx=-1)
    return z_part, zy_part, y_part, own, border


def classes_of(bias_table):
    table = bias_table.reshape(HEADS, 2 * WZ - 1, 2 * WY - 1, 2 * WX - 1)
    table = jnp.pad(table, ((0, 0), (1, 0), (1, 0), (1, 0)))
    table = table.reshape(HEADS, 2, WZ, 2, WY, 2, WX)
    return table.transpose(0, 1, 3, 5, 2, 4, 6).reshape(HEADS, 8, WT)


def swapped(value, axis, partners):
    return lax.ppermute(value, axis, list(enumerate(partners)))


def to_each(value, axes):
    count = lax.axis_size(axes)
    spread = jnp.broadcast_to(value[None], (count,) + value.shape)
    return lax.all_to_all(spread, axes, 0, 0, tiled=True)


def after(value, other):
    return lax.optimization_barrier((value, other))


def unshift_and_reduce(field, border, sums):
    half = ROWS // 2
    core = lax.axis_index("gx")
    mine = lax.dynamic_slice_in_dim(sums, core * half, half, 0)
    other = lax.dynamic_slice_in_dim(sums, (1 - core) * half, half, 0)
    mine = mine + swapped(other, "gx", (1, 0))
    border = sent(border, gx=1)[:, :, :SX]
    field = jnp.concatenate([border, field[:, :, SX:]], 2)
    y_border = sent(field[:, SY:], gy=1)
    count = lax.axis_size(PLANE)
    part = lax.all_to_all(mine.reshape(count, half // count, 128), PLANE, 0, 0, tiled=True).sum(0)
    part, field = after(part, field)
    part = to_each(part, "z").sum(0).astype(BF16)
    part, y_border = after(part, y_border)
    field = jnp.concatenate([y_border, field[:, :SY]], 1)
    z_border = sent(field[SZ:], gz=1)
    mine = to_each(part, PLANE).reshape(half, 128)
    outputs = finish(lax.all_gather(mine, "gx", axis=0, tiled=True))
    outputs, z_border = after(outputs, z_border)
    return jnp.concatenate([z_border, field[:SZ]], 0), *outputs


def per_device(tokens, ln_gain, ln_bias, qkv_weight, qkv_bias, proj_weight, bias_table, grad_out):
    count = tokens.shape[0] * tokens.shape[1] * tokens.shape[2]
    for axis in AXES:
        count *= lax.axis_size(axis)
    quarters = shift_pair(tokens, grad_out)
    w3 = qkv_weight.reshape(C, 3, C).transpose(1, 0, 2)
    w3t = qkv_weight.T.reshape(3, C, C)
    last = [lax.axis_index(a) == lax.axis_size(a) - 1 for a in AXES]
    flags = jnp.stack([last[0] & last[1], last[2], last[3]]).astype(jnp.int32)
    field, border, sums = windows(
        1.0 / math.sqrt(count),
        flags,
        *quarters,
        jnp.stack([ln_gain, ln_bias], 0),
        w3,
        w3t,
        qkv_bias.reshape(3, 1, C),
        qkv_bias.reshape(3, C, 1),
        proj_weight,
        classes_of(bias_table),
    )
    return unshift_and_reduce(field, border, sums)


def solution(mesh):
    sizes = mesh.devices.shape
    mesh = Mesh(mesh.devices.reshape(4, sizes[0] // 4, *sizes[1:]), AXES)
    grid = P(GZ, "gy", "gx", None)
    return jax.shard_map(
        per_device,
        mesh=mesh,
        in_specs=(grid, P(), P(), P(), P(), P(), P(), grid),
        out_specs=(grid, P(), P(), P(), P(), P(), P()),
        check_vma=False,
    )
```

```python
import functools
import math

import jax
import jax.numpy as jnp
import numpy as np
from jax import lax
from jax.experimental import pallas as pl
from jax.experimental.pallas import tpu as pltpu
from jax.sharding import Mesh
from jax.sharding import PartitionSpec as P

C = 192
HEADS = 6
HD = 32
WZ, WY, WX = 4, 8, 8
SZ, SY, SX = 2, 4, 4
WT = 256
TABLE = 1575
EPSILON = 1e-05
MASKED = -100.0
FACTOR = HD ** (-0.5)
GZ = ("yh", "z")
PLANE = ("yh", "gy")
AXES = ("yh", "z", "gy", "gx")
ROWS = 1536
TABLE_ROWS = 6 * C
USED = TABLE_ROWS + 128
F32 = jnp.float32
BF16 = jnp.bfloat16


def nn(a, b):
    return lax.dot_general(a, b, (((1,), (0,)), ((), ())), preferred_element_type=F32)


def nt(a, b):
    return lax.dot_general(a, b, (((1,), (1,)), ((), ())), preferred_element_type=F32)


def shifted(value, axis, steps):
    count = lax.axis_size(axis)
    pairs = [(source, (source + steps) % count) for source in range(count)]
    return lax.ppermute(value, axis, pairs)


def roll_lanes(value, steps):
    steps %= WT
    return value if steps == 0 else pltpu.roll(value, steps, 1)


def roll_rows_forward(value):
    return pltpu.roll(value, 0, 1, stride=1, stride_axis=0)


def iota(shape, dim):
    return lax.broadcasted_iota(jnp.int32, shape, dim)


def expand_bias(classes, lane):
    row = iota((8, WT), 0)
    z_slot, y_slot, x_slot = lane // 64, lane // 8 % 8, lane % 8
    by_x = {}
    for sz in range(2):
        for sy in range(2):
            at = sz * 4 + sy * 2
            below = jnp.broadcast_to(roll_lanes(classes[at : at + 1], -8), (8, WT))
            above = jnp.broadcast_to(classes[at + 1 : at + 2], (8, WT))
            by_x[sz, sy] = jnp.where(
                x_slot >= row, roll_rows_forward(above), roll_rows_forward(below)
            )
    parts = []
    for zk in range(WZ):
        by_z = [
            roll_lanes(jnp.where(z_slot < WZ - zk, by_x[1, sy], by_x[0, sy]), 64 * zk)
            for sy in range(2)
        ]
        below = roll_lanes(by_z[0], -64)
        for yk in range(WY):
            parts.append(roll_lanes(jnp.where(y_slot < WY - yk, by_z[1], below), 8 * yk))
    return jnp.concatenate(parts, 0)


def collect_bias(pair_sums, lane):
    row = iota((8, WT), 0)
    z_slot, y_slot, x_slot = lane // 64, lane // 8 % 8, lane % 8
    by_z = [[None, None], [None, None]]
    for zk in range(WZ):
        above = below = None
        for yk in range(WY):
            at = (zk * WY + yk) * WX
            part = roll_lanes(pair_sums[at : at + 8], -8 * yk)
            stays = y_slot < WY - yk
            up = jnp.where(stays, part, 0.0)
            above = up if above is None else above + up
            if yk:
                down = jnp.where(stays, 0.0, part)
                below = down if below is None else below + down
        below = roll_lanes(below, 64)
        stays = z_slot < WZ - zk
        for sy, value in enumerate((below, above)):
            value = roll_lanes(value, -64 * zk)
            for sz, term in enumerate((jnp.where(stays, 0.0, value), jnp.where(stays, value, 0.0))):
                old = by_z[sz][sy]
                by_z[sz][sy] = term if old is None else old + term
    out = []
    for sz in range(2):
        for sy in range(2):
            value = by_z[sz][sy]
            turned = value
            for xk in range(1, WX):
                turned = jnp.where(row == xk, roll_lanes(value, -xk), turned)
            stays = x_slot < WX - row
            out.append(roll_lanes(jnp.sum(jnp.where(stays, 0.0, turned), 0, keepdims=True), 8))
            out.append(jnp.sum(jnp.where(stays, turned, 0.0), 0, keepdims=True))
    return jnp.concatenate(out, 0)


def block_of(own, y_part, z_part, zy_part):
    near, far = (
        jnp.concatenate([ref[...].astype(F32) for ref in pair], 1)
        for pair in ((own, y_part), (z_part, zy_part))
    )
    return jnp.concatenate([near, far], 0).reshape(WZ * WY, 16, 2 * C)


def windows_of(block, border):
    first, second = block[:, :8], block[:, 8:]
    border = jnp.concatenate([border, border], 1)
    early = iota((WZ * WY, 8, 2 * C), 1) < SX
    return [
        pltpu.roll(jnp.where(early, right, left), SX, 1).reshape(WT, 2 * C)
        for left, right in ((first, second), (second, border))
    ]


def columns_of(windows):
    early = iota((WZ * WY, 8, C), 1) < SX
    first, second = (pltpu.roll(w.reshape(WZ * WY, 8, C), SX, 1) for w in windows)
    block = jnp.concatenate([first, jnp.where(early, first, second)], 1)
    return block.reshape(WZ, WY, 16, C), second.reshape(WZ, WY, 8, C)


def kernel(
    scale,
    flags_ref,
    z_ref,
    zy_ref,
    y_ref,
    own_ref,
    border_ref,
    norm_ref,
    w_ref,
    wt_ref,
    qkv_bias_ref,
    qkv_bias_t_ref,
    proj_ref,
    table_ref,
    grad_ref,
    border_grad_ref,
    sums_ref,
    xhat_s,
    rstd_s,
    normed_s,
    cot_s,
    qkv_s,
    qkvt_s,
    datt_s,
    dattt_s,
    attt_s,
    dqt_s,
    dkv_s,
    pen_s,
    table_s,
):
    gain = norm_ref[0:1, :]
    beta = norm_ref[1:2, :]
    lane = iota((8, WT), 1)
    lane_row = iota((1, WT), 1)
    sub_col = iota((WT, 1), 0)

    block = block_of(own_ref, y_ref, z_ref, zy_ref)
    border = jnp.concatenate([border_ref[SZ:], border_ref[:SZ]], 0).astype(F32)
    both = windows_of(block, border.reshape(WZ * WY, SX, 2 * C))
    for w in range(2):
        tok = both[w][:, :C]
        cot = both[w][:, C:].astype(BF16)
        mean = jnp.mean(tok, -1, keepdims=True)
        centred = tok - mean
        rstd = lax.rsqrt(jnp.mean(centred * centred, -1, keepdims=True) + EPSILON)
        xhat = centred * rstd
        normed = (xhat * gain + beta).astype(BF16)
        xhat_s[w] = xhat
        rstd_s[w] = rstd
        normed_s[w] = normed
        cot_s[w] = cot
        for p in range(3):
            qkv_s[w, p] = (nn(normed, w_ref[p]) + qkv_bias_ref[p]).astype(BF16)
            qkvt_s[w, p] = (nt(wt_ref[p], normed) + qkv_bias_t_ref[p]).astype(BF16)
        datt_s[w] = nt(cot, proj_ref[...]).astype(BF16)
        dattt_s[w] = nt(proj_ref[...], cot).astype(BF16)

        fz, fy = flags_ref[0], flags_ref[1]
        fx = flags_ref[2] if w else 0

        def code(t):
            half = (t // 128) * fz * 4 + (t // 32 % 2) * fy * 2
            return half + (t // 4 % 2) * fx if w else half

        pen_s[w] = jnp.where(code(sub_col) == code(lane_row), 0.0, MASKED).astype(F32)

    for h in range(HEADS):
        bias = expand_bias(table_ref[h], lane)
        pair_sums = None
        part = slice(HD * h, HD * h + HD)
        for w in range(2):
            query, keys, values = (qkv_s[w, p, :, part] for p in range(3))
            query_t, keys_t, values_t = (qkvt_s[w, p, part, :] for p in range(3))
            d_att = datt_s[w, :, part]
            d_att_t = dattt_s[w, part, :]
            scores = nn(keys, query_t) * FACTOR + bias + pen_s[w]
            exponent = jnp.exp(scores - jnp.max(scores, 0, keepdims=True))
            probs = exponent * (1.0 / jnp.sum(exponent, 0, keepdims=True))
            probs_b = probs.astype(BF16)
            attt_s[w, part, :] = nn(values_t, probs_b).astype(BF16)
            d_probs = nn(values, d_att_t)
            dkv_s[w, 1, :, part] = nn(probs_b, d_att).astype(BF16)
            d_scores = probs * (d_probs - jnp.sum(probs * d_probs, 0, keepdims=True))
            d_scores_b = d_scores.astype(BF16)
            dqt_s[w, part, :] = nn(keys_t, d_scores_b) * FACTOR
            dkv_s[w, 0, :, part] = (nn(d_scores_b, query) * FACTOR).astype(BF16)
            pair_sums = d_scores if pair_sums is None else pair_sums + d_scores
        found = collect_bias(pair_sums, lane)
        for c in range(8):
            table_s[c, h : h + 1, :] = found[c : c + 1]

    totals = [None] * 4
    vectors = [None] * 5
    grads = []

    def add(store, at, term):
        store[at] = term if store[at] is None else store[at] + term

    for w in range(2):
        normed = normed_s[w]
        normed_t = normed.astype(F32).T.astype(BF16)
        cot = cot_s[w]
        d_query = dqt_s[w].T.astype(BF16)
        d_normed = None
        for p, d_part in enumerate((d_query, dkv_s[w, 0], dkv_s[w, 1])):
            add(totals, p, nn(normed_t, d_part))
            add(vectors, p, jnp.sum(d_part.astype(F32), 0, keepdims=True))
            term = nn(d_part, wt_ref[p])
            d_normed = term if d_normed is None else d_normed + term
        add(totals, 3, nn(attt_s[w], cot))
        xhat = xhat_s[w]
        add(vectors, 3, jnp.sum(d_normed * xhat, 0, keepdims=True))
        add(vectors, 4, jnp.sum(d_normed, 0, keepdims=True))
        d_xhat = d_normed * gain
        first = jnp.mean(d_xhat, -1, keepdims=True)
        second = jnp.mean(d_xhat * xhat, -1, keepdims=True)
        grad = cot.astype(F32) + rstd_s[w] * (d_xhat - first - xhat * second)
        grads.append(grad)

    block, border = columns_of(grads)
    grad_ref[...] = block.astype(BF16)
    border_grad_ref[...] = border.astype(BF16)
    for p in range(4):
        sums_ref[C * p : C * p + C, :] = totals[p][:, :128] * scale
    for p in range(2):
        rest = [totals[2 * p][:, 128:], totals[2 * p + 1][:, 128:]]
        sums_ref[C * (4 + p) : C * (5 + p), :] = jnp.concatenate(rest, 1) * scale
    for c in range(8):
        table_s[c, 6:, :] = jnp.zeros((2, WT), F32)
        if c < 5:
            table_s[c, 6:7, :C] = vectors[c]
        sums_ref[TABLE_ROWS + 16 * c : TABLE_ROWS + 16 * c + 8, :] = table_s[c, :, :128] * scale
        sums_ref[TABLE_ROWS + 16 * c + 8 : TABLE_ROWS + 16 * c + 16, :] = table_s[c, :, 128:] * scale
    sums_ref[USED:, :] = jnp.zeros((ROWS - USED, 128), F32)


def finish_kernel(sums_ref, gain_ref, shift_ref, qkv_ref, bias_ref, proj_ref, table_ref):
    firsts = [sums_ref[C * p : C * p + C, :].astype(F32) for p in range(4)]
    rests = [sums_ref[C * (4 + p) : C * (5 + p), :].astype(F32) for p in range(2)]
    parts = []
    for p in range(4):
        rest = rests[p // 2]
        parts += [firsts[p], rest[:, :64] if p % 2 == 0 else rest[:, 64:]]
    qkv_ref[...] = jnp.concatenate(parts[:6], 1)
    proj_ref[...] = jnp.concatenate(parts[6:], 1)
    classes = []
    for c in range(8):
        at = TABLE_ROWS + 16 * c
        pair = sums_ref[at : at + 16, :].astype(F32)
        classes.append(jnp.concatenate([pair[:8], pair[8:]], 1))
    vectors = [classes[c][6:7, :C] for c in range(5)]
    bias_ref[...] = jnp.concatenate(vectors[:3], 1)[0]
    gain_ref[...] = vectors[3][0]
    shift_ref[...] = vectors[4][0]
    block = iota((8, WT), 1) // 64
    rows = []
    for index in range(1, 2 * WZ):
        sz, z = index // WZ, index % WZ
        joined = None
        for j in range(4):
            term = roll_lanes(classes[4 * sz + j], 64 * (j - z))
            joined = term if joined is None else jnp.where(block == j, term, joined)
        rows.append(joined)
    source = iota((WT, WT), 0)
    dy = source // 8 % 8 + (source // 128) * 8 - 8
    dx = source % 8 + (source // 64 % 2) * 8 - 8
    target = jnp.where((dy > -8) & (dx > -8), (dy + 7) * 15 + dx + 7, -1)
    pick = (target == iota((WT, WT), 1)).astype(F32)
    placed = lax.dot_general(
        jnp.concatenate(rows, 0),
        pick,
        (((1,), (0,)), ((), ())),
        precision=lax.Precision.HIGHEST,
        preferred_element_type=F32,
    )
    table_ref[...] = jnp.concatenate(
        [placed[8 * d : 8 * d + HEADS, :225] for d in range(2 * WZ - 1)], 1
    )


def finish(sums):
    vmem = pl.BlockSpec(memory_space=pltpu.VMEM)
    return pl.pallas_call(
        finish_kernel,
        out_shape=tuple(
            jax.ShapeDtypeStruct(shape, F32)
            for shape in ((C,), (C,), (C, 3 * C), (3 * C,), (C, C), (HEADS, TABLE))
        ),
        in_specs=[vmem],
        out_specs=(vmem,) * 6,
        compiler_params=pltpu.CompilerParams(vmem_limit_bytes=16 * 1024 * 1024),
        name="finish",
    )(sums)


def windows(scale, *operands):
    vmem = pl.BlockSpec(memory_space=pltpu.VMEM)
    return pl.pallas_call(
        functools.partial(kernel, scale),
        out_shape=(
            jax.ShapeDtypeStruct((WZ, WY, 16, C), BF16),
            jax.ShapeDtypeStruct((WZ, WY, 8, C), BF16),
            jax.ShapeDtypeStruct((ROWS, 128), F32),
        ),
        in_specs=[pl.BlockSpec(memory_space=pltpu.SMEM)] + [vmem] * (len(operands) - 1),
        out_specs=(vmem,) * 3,
        scratch_shapes=[
            pltpu.VMEM((2, WT, C), F32),
            pltpu.VMEM((2, WT, 1), F32),
            pltpu.VMEM((2, WT, C), BF16),
            pltpu.VMEM((2, WT, C), BF16),
            pltpu.VMEM((2, 3, WT, C), BF16),
            pltpu.VMEM((2, 3, C, WT), BF16),
            pltpu.VMEM((2, WT, C), BF16),
            pltpu.VMEM((2, C, WT), BF16),
            pltpu.VMEM((2, C, WT), BF16),
            pltpu.VMEM((2, C, WT), F32),
            pltpu.VMEM((2, 2, WT, C), BF16),
            pltpu.VMEM((2, WT, WT), F32),
            pltpu.VMEM((8, 8, WT), F32),
        ],
        compiler_params=pltpu.CompilerParams(vmem_limit_bytes=48 * 1024 * 1024),
        cost_estimate=pl.CostEstimate(
            flops=1_000_000_000, bytes_accessed=3_000_000, transcendentals=800_000
        ),
        name="windows",
    )(*operands)


def sent(value, gz=0, gy=0, gx=0):
    axes, sizes, steps = [], [], []
    for names, step in ((GZ, gz), (("gy",), gy), (("gx",), gx)):
        if step:
            axes += names
            sizes.append(math.prod(lax.axis_size(a) for a in names))
            steps.append(step)
    pairs = []
    for place in np.ndindex(*sizes):
        to = tuple((p + s) % n for p, s, n in zip(place, steps, sizes))
        pairs.append(tuple(int(np.ravel_multi_index(q, sizes)) for q in (place, to)))
    return lax.ppermute(value, tuple(axes), pairs)


def shift_pair(tokens, grad_out):
    both = jnp.concatenate([tokens, grad_out], -1)
    z_part = sent(both[:SZ, SY:], gz=-1)
    zy_part = sent(both[:SZ, :SY], gz=-1, gy=-1)
    y_part = sent(both[SZ:, :SY], gy=-1)
    own = both[SZ:, SY:]
    far, near = (
        jnp.concatenate([v[:, :, :SX] for v in pair], 1)
        for pair in ((z_part, zy_part), (own, y_part))
    )
    border = sent(jnp.concatenate([far, near], 0), gx=-1)
    return z_part, zy_part, y_part, own, border


def classes_of(bias_table):
    table = bias_table.reshape(HEADS, 2 * WZ - 1, 2 * WY - 1, 2 * WX - 1)
    table = jnp.pad(table, ((0, 0), (1, 0), (1, 0), (1, 0)))
    table = table.reshape(HEADS, 2, WZ, 2, WY, 2, WX)
    return table.transpose(0, 1, 3, 5, 2, 4, 6).reshape(HEADS, 8, WT)


def swapped(value, axis, partners):
    return lax.ppermute(value, axis, list(enumerate(partners)))


def to_each(value, axes):
    count = lax.axis_size(axes)
    spread = jnp.broadcast_to(value[None], (count,) + value.shape)
    return lax.all_to_all(spread, axes, 0, 0, tiled=True)


def after(value, other):
    return lax.optimization_barrier((value, other))


def unshift_and_reduce(field, border, sums):
    half = ROWS // 2
    core = lax.axis_index("gx")
    mine = lax.dynamic_slice_in_dim(sums, core * half, half, 0)
    other = lax.dynamic_slice_in_dim(sums, (1 - core) * half, half, 0)
    mine = (mine + swapped(other, "gx", (1, 0))).astype(BF16)
    border = sent(border, gx=1)[:, :, :SX]
    field = jnp.concatenate([border, field[:, :, SX:]], 2)
    y_border = sent(field[:, SY:], gy=1)
    count = lax.axis_size(PLANE)
    part = lax.all_to_all(mine.reshape(count, half // count, 128), PLANE, 0, 0, tiled=True)
    part = part.astype(F32).sum(0)
    part, field = after(part, field)
    part = to_each(part, "z").sum(0)
    part, y_border = after(part, y_border)
    field = jnp.concatenate([y_border, field[:, :SY]], 1)
    z_border = sent(field[SZ:], gz=1)
    mine = to_each(part, PLANE).reshape(half, 128)
    outputs = finish(lax.all_gather(mine, "gx", axis=0, tiled=True))
    outputs, z_border = after(outputs, z_border)
    return jnp.concatenate([z_border, field[:SZ]], 0), *outputs


def per_device(tokens, ln_gain, ln_bias, qkv_weight, qkv_bias, proj_weight, bias_table, grad_out):
    count = tokens.shape[0] * tokens.shape[1] * tokens.shape[2]
    for axis in AXES:
        count *= lax.axis_size(axis)
    quarters = shift_pair(tokens, grad_out)
    w3 = qkv_weight.reshape(C, 3, C).transpose(1, 0, 2)
    w3t = qkv_weight.T.reshape(3, C, C)
    last = [lax.axis_index(a) == lax.axis_size(a) - 1 for a in AXES]
    flags = jnp.stack([last[0] & last[1], last[2], last[3]]).astype(jnp.int32)
    field, border, sums = windows(
        1.0 / math.sqrt(count),
        flags,
        *quarters,
        jnp.stack([ln_gain, ln_bias], 0),
        w3,
        w3t,
        qkv_bias.reshape(3, 1, C),
        qkv_bias.reshape(3, C, 1),
        proj_weight,
        classes_of(bias_table),
    )
    return unshift_and_reduce(field, border, sums)


def solution(mesh):
    sizes = mesh.devices.shape
    mesh = Mesh(mesh.devices.reshape(4, sizes[0] // 4, *sizes[1:]), AXES)
    grid = P(GZ, "gy", "gx", None)
    return jax.shard_map(
        per_device,
        mesh=mesh,
        in_specs=(grid, P(), P(), P(), P(), P(), P(), grid),
        out_specs=(grid, P(), P(), P(), P(), P(), P()),
        check_vma=False,
    )
```

```python
import functools
import math

import jax
import jax.numpy as jnp
import numpy as np
from jax import lax
from jax.experimental import pallas as pl
from jax.experimental.pallas import tpu as pltpu
from jax.sharding import Mesh
from jax.sharding import PartitionSpec as P

C = 192
HEADS = 6
HD = 32
WZ, WY, WX = 4, 8, 8
SZ, SY, SX = 2, 4, 4
WT = 256
TABLE = 1575
EPSILON = 1e-05
MASKED = -100.0
FACTOR = HD ** (-0.5)
GZ = ("yh", "z")
PLANE = ("yh", "gy")
AXES = ("yh", "z", "gy", "gx")
ROWS = 1536
TABLE_ROWS = 6 * C
USED = TABLE_ROWS + 128
F32 = jnp.float32
BF16 = jnp.bfloat16


def nn(a, b):
    return lax.dot_general(a, b, (((1,), (0,)), ((), ())), preferred_element_type=F32)


def nt(a, b):
    return lax.dot_general(a, b, (((1,), (1,)), ((), ())), preferred_element_type=F32)


def shifted(value, axis, steps):
    count = lax.axis_size(axis)
    pairs = [(source, (source + steps) % count) for source in range(count)]
    return lax.ppermute(value, axis, pairs)


def roll_lanes(value, steps):
    steps %= WT
    return value if steps == 0 else pltpu.roll(value, steps, 1)


def roll_rows_forward(value):
    return pltpu.roll(value, 0, 1, stride=1, stride_axis=0)


def iota(shape, dim):
    return lax.broadcasted_iota(jnp.int32, shape, dim)


def expand_bias(classes, lane):
    row = iota((8, WT), 0)
    z_slot, y_slot, x_slot = lane // 64, lane // 8 % 8, lane % 8
    by_x = {}
    for sz in range(2):
        for sy in range(2):
            at = sz * 4 + sy * 2
            below = jnp.broadcast_to(roll_lanes(classes[at : at + 1], -8), (8, WT))
            above = jnp.broadcast_to(classes[at + 1 : at + 2], (8, WT))
            by_x[sz, sy] = jnp.where(
                x_slot >= row, roll_rows_forward(above), roll_rows_forward(below)
            )
    parts = []
    for zk in range(WZ):
        by_z = [
            roll_lanes(jnp.where(z_slot < WZ - zk, by_x[1, sy], by_x[0, sy]), 64 * zk)
            for sy in range(2)
        ]
        below = roll_lanes(by_z[0], -64)
        for yk in range(WY):
            parts.append(roll_lanes(jnp.where(y_slot < WY - yk, by_z[1], below), 8 * yk))
    return jnp.concatenate(parts, 0)


def collect_bias(pair_sums, lane):
    row = iota((8, WT), 0)
    z_slot, y_slot, x_slot = lane // 64, lane // 8 % 8, lane % 8
    by_z = [[None, None], [None, None]]
    for zk in range(WZ):
        above = below = None
        for yk in range(WY):
            at = (zk * WY + yk) * WX
            part = roll_lanes(pair_sums[at : at + 8], -8 * yk)
            stays = y_slot < WY - yk
            up = jnp.where(stays, part, 0.0)
            above = up if above is None else above + up
            if yk:
                down = jnp.where(stays, 0.0, part)
                below = down if below is None else below + down
        below = roll_lanes(below, 64)
        stays = z_slot < WZ - zk
        for sy, value in enumerate((below, above)):
            value = roll_lanes(value, -64 * zk)
            for sz, term in enumerate((jnp.where(stays, 0.0, value), jnp.where(stays, value, 0.0))):
                old = by_z[sz][sy]
                by_z[sz][sy] = term if old is None else old + term
    out = []
    for sz in range(2):
        for sy in range(2):
            value = by_z[sz][sy]
            turned = value
            for xk in range(1, WX):
                turned = jnp.where(row == xk, roll_lanes(value, -xk), turned)
            stays = x_slot < WX - row
            out.append(roll_lanes(jnp.sum(jnp.where(stays, 0.0, turned), 0, keepdims=True), 8))
            out.append(jnp.sum(jnp.where(stays, turned, 0.0), 0, keepdims=True))
    return jnp.concatenate(out, 0)


def block_of(own, y_part, z_part, zy_part):
    near, far = (
        jnp.concatenate([ref[...].astype(F32) for ref in pair], 1)
        for pair in ((own, y_part), (z_part, zy_part))
    )
    return jnp.concatenate([near, far], 0).reshape(WZ * WY, 16, 2 * C)


def windows_of(block, border):
    first, second = block[:, :8], block[:, 8:]
    border = jnp.concatenate([border, border], 1)
    early = iota((WZ * WY, 8, 2 * C), 1) < SX
    return [
        pltpu.roll(jnp.where(early, right, left), SX, 1).reshape(WT, 2 * C)
        for left, right in ((first, second), (second, border))
    ]


def columns_of(windows):
    early = iota((WZ * WY, 8, C), 1) < SX
    first, second = (pltpu.roll(w.reshape(WZ * WY, 8, C), SX, 1) for w in windows)
    block = jnp.concatenate([first, jnp.where(early, first, second)], 1)
    return block.reshape(WZ, WY, 16, C), second.reshape(WZ, WY, 8, C)


def kernel(
    scale,
    flags_ref,
    z_ref,
    zy_ref,
    y_ref,
    own_ref,
    border_ref,
    norm_ref,
    w_ref,
    wt_ref,
    qkv_bias_ref,
    qkv_bias_t_ref,
    proj_ref,
    table_ref,
    grad_ref,
    border_grad_ref,
    sums_ref,
    xhat_s,
    rstd_s,
    normed_s,
    cot_s,
    qkv_s,
    qkvt_s,
    datt_s,
    dattt_s,
    attt_s,
    dqt_s,
    dkv_s,
    pen_s,
    table_s,
):
    gain = norm_ref[0:1, :]
    beta = norm_ref[1:2, :]
    lane = iota((8, WT), 1)
    lane_row = iota((1, WT), 1)
    sub_col = iota((WT, 1), 0)

    block = block_of(own_ref, y_ref, z_ref, zy_ref)
    border = jnp.concatenate([border_ref[SZ:], border_ref[:SZ]], 0).astype(F32)
    both = windows_of(block, border.reshape(WZ * WY, SX, 2 * C))
    for w in range(2):
        tok = both[w][:, :C]
        cot = both[w][:, C:].astype(BF16)
        mean = jnp.mean(tok, -1, keepdims=True)
        centred = tok - mean
        rstd = lax.rsqrt(jnp.mean(centred * centred, -1, keepdims=True) + EPSILON)
        xhat = centred * rstd
        normed = (xhat * gain + beta).astype(BF16)
        xhat_s[w] = xhat
        rstd_s[w] = rstd
        normed_s[w] = normed
        cot_s[w] = cot
        for p in range(3):
            qkv_s[w, p] = (nn(normed, w_ref[p]) + qkv_bias_ref[p]).astype(BF16)
            qkvt_s[w, p] = (nt(wt_ref[p], normed) + qkv_bias_t_ref[p]).astype(BF16)
        datt_s[w] = nt(cot, proj_ref[...]).astype(BF16)
        dattt_s[w] = nt(proj_ref[...], cot).astype(BF16)

        fz, fy = flags_ref[0], flags_ref[1]
        fx = flags_ref[2] if w else 0

        def code(t):
            half = (t // 128) * fz * 4 + (t // 32 % 2) * fy * 2
            return half + (t // 4 % 2) * fx if w else half

        pen_s[w] = jnp.where(code(sub_col) == code(lane_row), 0.0, MASKED).astype(F32)

    for h in range(HEADS):
        bias = expand_bias(table_ref[h], lane)
        pair_sums = None
        part = slice(HD * h, HD * h + HD)
        for w in range(2):
            query, keys, values = (qkv_s[w, p, :, part] for p in range(3))
            query_t, keys_t, values_t = (qkvt_s[w, p, part, :] for p in range(3))
            d_att = datt_s[w, :, part]
            d_att_t = dattt_s[w, part, :]
            scores = nn(keys, query_t) * FACTOR + bias + pen_s[w]
            exponent = jnp.exp(scores - jnp.max(scores, 0, keepdims=True))
            probs = exponent * (1.0 / jnp.sum(exponent, 0, keepdims=True))
            probs_b = probs.astype(BF16)
            attt_s[w, part, :] = nn(values_t, probs_b).astype(BF16)
            d_probs = nn(values, d_att_t)
            dkv_s[w, 1, :, part] = nn(probs_b, d_att).astype(BF16)
            d_scores = probs * (d_probs - jnp.sum(probs * d_probs, 0, keepdims=True))
            d_scores_b = d_scores.astype(BF16)
            dqt_s[w, part, :] = nn(keys_t, d_scores_b) * FACTOR
            dkv_s[w, 0, :, part] = (nn(d_scores_b, query) * FACTOR).astype(BF16)
            pair_sums = d_scores if pair_sums is None else pair_sums + d_scores
        found = collect_bias(pair_sums, lane)
        for c in range(8):
            table_s[c, h : h + 1, :] = found[c : c + 1]

    totals = [None] * 4
    vectors = [None] * 5
    grads = []

    def add(store, at, term):
        store[at] = term if store[at] is None else store[at] + term

    for w in range(2):
        normed = normed_s[w]
        normed_t = normed.astype(F32).T.astype(BF16)
        cot = cot_s[w]
        d_query = dqt_s[w].T.astype(BF16)
        d_normed = None
        for p, d_part in enumerate((d_query, dkv_s[w, 0], dkv_s[w, 1])):
            add(totals, p, nn(normed_t, d_part))
            add(vectors, p, jnp.sum(d_part.astype(F32), 0, keepdims=True))
            term = nn(d_part, wt_ref[p])
            d_normed = term if d_normed is None else d_normed + term
        add(totals, 3, nn(attt_s[w], cot))
        xhat = xhat_s[w]
        add(vectors, 3, jnp.sum(d_normed * xhat, 0, keepdims=True))
        add(vectors, 4, jnp.sum(d_normed, 0, keepdims=True))
        d_xhat = d_normed * gain
        first = jnp.mean(d_xhat, -1, keepdims=True)
        second = jnp.mean(d_xhat * xhat, -1, keepdims=True)
        grad = cot.astype(F32) + rstd_s[w] * (d_xhat - first - xhat * second)
        grads.append(grad)

    block, border = columns_of(grads)
    grad_ref[...] = block.astype(BF16)
    border_grad_ref[...] = border.astype(BF16)
    for p in range(4):
        sums_ref[C * p : C * p + C, :] = totals[p][:, :128] * scale
    for p in range(2):
        rest = [totals[2 * p][:, 128:], totals[2 * p + 1][:, 128:]]
        sums_ref[C * (4 + p) : C * (5 + p), :] = jnp.concatenate(rest, 1) * scale
    for c in range(8):
        table_s[c, 6:, :] = jnp.zeros((2, WT), F32)
        if c < 5:
            table_s[c, 6:7, :C] = vectors[c]
        sums_ref[TABLE_ROWS + 16 * c : TABLE_ROWS + 16 * c + 8, :] = table_s[c, :, :128] * scale
        sums_ref[TABLE_ROWS + 16 * c + 8 : TABLE_ROWS + 16 * c + 16, :] = table_s[c, :, 128:] * scale
    sums_ref[USED:, :] = jnp.zeros((ROWS - USED, 128), F32)


def finish_kernel(sums_ref, gain_ref, shift_ref, qkv_ref, bias_ref, proj_ref, table_ref):
    firsts = [sums_ref[C * p : C * p + C, :].astype(F32) for p in range(4)]
    rests = [sums_ref[C * (4 + p) : C * (5 + p), :].astype(F32) for p in range(2)]
    parts = []
    for p in range(4):
        rest = rests[p // 2]
        parts += [firsts[p], rest[:, :64] if p % 2 == 0 else rest[:, 64:]]
    qkv_ref[...] = jnp.concatenate(parts[:6], 1)
    proj_ref[...] = jnp.concatenate(parts[6:], 1)
    classes = []
    for c in range(8):
        at = TABLE_ROWS + 16 * c
        pair = sums_ref[at : at + 16, :].astype(F32)
        classes.append(jnp.concatenate([pair[:8], pair[8:]], 1))
    vectors = [classes[c][6:7, :C] for c in range(5)]
    bias_ref[...] = jnp.concatenate(vectors[:3], 1)[0]
    gain_ref[...] = vectors[3][0]
    shift_ref[...] = vectors[4][0]
    block = iota((8, WT), 1) // 64
    rows = []
    for index in range(1, 2 * WZ):
        sz, z = index // WZ, index % WZ
        joined = None
        for j in range(4):
            term = roll_lanes(classes[4 * sz + j], 64 * (j - z))
            joined = term if joined is None else jnp.where(block == j, term, joined)
        rows.append(joined)
    source = iota((WT, WT), 0)
    dy = source // 8 % 8 + (source // 128) * 8 - 8
    dx = source % 8 + (source // 64 % 2) * 8 - 8
    target = jnp.where((dy > -8) & (dx > -8), (dy + 7) * 15 + dx + 7, -1)
    pick = (target == iota((WT, WT), 1)).astype(F32)
    placed = lax.dot_general(
        jnp.concatenate(rows, 0),
        pick,
        (((1,), (0,)), ((), ())),
        precision=lax.Precision.HIGHEST,
        preferred_element_type=F32,
    )
    table_ref[...] = jnp.concatenate(
        [placed[8 * d : 8 * d + HEADS, :225] for d in range(2 * WZ - 1)], 1
    )


def finish(sums):
    vmem = pl.BlockSpec(memory_space=pltpu.VMEM)
    return pl.pallas_call(
        finish_kernel,
        out_shape=tuple(
            jax.ShapeDtypeStruct(shape, F32)
            for shape in ((C,), (C,), (C, 3 * C), (3 * C,), (C, C), (HEADS, TABLE))
        ),
        in_specs=[vmem],
        out_specs=(vmem,) * 6,
        compiler_params=pltpu.CompilerParams(vmem_limit_bytes=16 * 1024 * 1024),
        name="finish",
    )(sums)


def windows(scale, *operands):
    vmem = pl.BlockSpec(memory_space=pltpu.VMEM)
    return pl.pallas_call(
        functools.partial(kernel, scale),
        out_shape=(
            jax.ShapeDtypeStruct((WZ, WY, 16, C), BF16),
            jax.ShapeDtypeStruct((WZ, WY, 8, C), BF16),
            jax.ShapeDtypeStruct((ROWS, 128), F32),
        ),
        in_specs=[pl.BlockSpec(memory_space=pltpu.SMEM)] + [vmem] * (len(operands) - 1),
        out_specs=(vmem,) * 3,
        scratch_shapes=[
            pltpu.VMEM((2, WT, C), F32),
            pltpu.VMEM((2, WT, 1), F32),
            pltpu.VMEM((2, WT, C), BF16),
            pltpu.VMEM((2, WT, C), BF16),
            pltpu.VMEM((2, 3, WT, C), BF16),
            pltpu.VMEM((2, 3, C, WT), BF16),
            pltpu.VMEM((2, WT, C), BF16),
            pltpu.VMEM((2, C, WT), BF16),
            pltpu.VMEM((2, C, WT), BF16),
            pltpu.VMEM((2, C, WT), F32),
            pltpu.VMEM((2, 2, WT, C), BF16),
            pltpu.VMEM((2, WT, WT), F32),
            pltpu.VMEM((8, 8, WT), F32),
        ],
        compiler_params=pltpu.CompilerParams(vmem_limit_bytes=48 * 1024 * 1024),
        cost_estimate=pl.CostEstimate(
            flops=1_000_000_000, bytes_accessed=3_000_000, transcendentals=800_000
        ),
        name="windows",
    )(*operands)


def sent(value, gz=0, gy=0, gx=0):
    axes, sizes, steps = [], [], []
    for names, step in ((GZ, gz), (("gy",), gy), (("gx",), gx)):
        if step:
            axes += names
            sizes.append(math.prod(lax.axis_size(a) for a in names))
            steps.append(step)
    pairs = []
    for place in np.ndindex(*sizes):
        to = tuple((p + s) % n for p, s, n in zip(place, steps, sizes))
        pairs.append(tuple(int(np.ravel_multi_index(q, sizes)) for q in (place, to)))
    return lax.ppermute(value, tuple(axes), pairs)


def shift_pair(tokens, grad_out):
    both = jnp.concatenate([tokens, grad_out], -1)
    z_part = sent(both[:SZ, SY:], gz=-1)
    zy_part = sent(both[:SZ, :SY], gz=-1, gy=-1)
    y_part = sent(both[SZ:, :SY], gy=-1)
    own = both[SZ:, SY:]
    far, near = (
        jnp.concatenate([v[:, :, :SX] for v in pair], 1)
        for pair in ((z_part, zy_part), (own, y_part))
    )
    border = sent(jnp.concatenate([far, near], 0), gx=-1)
    return z_part, zy_part, y_part, own, border


def classes_of(bias_table):
    table = bias_table.reshape(HEADS, 2 * WZ - 1, 2 * WY - 1, 2 * WX - 1)
    table = jnp.pad(table, ((0, 0), (1, 0), (1, 0), (1, 0)))
    table = table.reshape(HEADS, 2, WZ, 2, WY, 2, WX)
    return table.transpose(0, 1, 3, 5, 2, 4, 6).reshape(HEADS, 8, WT)


def swapped(value, axis, partners):
    return lax.ppermute(value, axis, list(enumerate(partners)))


def to_each(value, axes):
    count = lax.axis_size(axes)
    spread = jnp.broadcast_to(value[None], (count,) + value.shape)
    return lax.all_to_all(spread, axes, 0, 0, tiled=True)


def after(value, other):
    return lax.optimization_barrier((value, other))


def unshift_and_reduce(field, border, sums):
    half = ROWS // 2
    core = lax.axis_index("gx")
    mine = lax.dynamic_slice_in_dim(sums, core * half, half, 0)
    other = lax.dynamic_slice_in_dim(sums, (1 - core) * half, half, 0)
    mine = (mine + swapped(other, "gx", (1, 0))).astype(BF16)
    mine, border = after(mine, sent(border, gx=1)[:, :, :SX])
    field = jnp.concatenate([border, field[:, :, SX:]], 2)
    y_border = sent(field[:, SY:], gy=1)
    count = lax.axis_size(PLANE)
    part = lax.all_to_all(mine.reshape(count, half // count, 128), PLANE, 0, 0, tiled=True)
    part = part.astype(F32).sum(0)
    part, field = after(part, field)
    part = to_each(part, "z").sum(0)
    part, y_border = after(part, y_border)
    field = jnp.concatenate([y_border, field[:, :SY]], 1)
    z_border = sent(field[SZ:], gz=1)
    mine = to_each(part, PLANE).reshape(half, 128)
    outputs = finish(lax.all_gather(mine, "gx", axis=0, tiled=True))
    outputs, z_border = after(outputs, z_border)
    return jnp.concatenate([z_border, field[:SZ]], 0), *outputs


def per_device(tokens, ln_gain, ln_bias, qkv_weight, qkv_bias, proj_weight, bias_table, grad_out):
    count = tokens.shape[0] * tokens.shape[1] * tokens.shape[2]
    for axis in AXES:
        count *= lax.axis_size(axis)
    quarters = shift_pair(tokens, grad_out)
    w3 = qkv_weight.reshape(C, 3, C).transpose(1, 0, 2)
    w3t = qkv_weight.T.reshape(3, C, C)
    last = [lax.axis_index(a) == lax.axis_size(a) - 1 for a in AXES]
    flags = jnp.stack([last[0] & last[1], last[2], last[3]]).astype(jnp.int32)
    field, border, sums = windows(
        1.0 / math.sqrt(count),
        flags,
        *quarters,
        jnp.stack([ln_gain, ln_bias], 0),
        w3,
        w3t,
        qkv_bias.reshape(3, 1, C),
        qkv_bias.reshape(3, C, 1),
        proj_weight,
        classes_of(bias_table),
    )
    return unshift_and_reduce(field, border, sums)


def solution(mesh):
    sizes = mesh.devices.shape
    mesh = Mesh(mesh.devices.reshape(4, sizes[0] // 4, *sizes[1:]), AXES)
    grid = P(GZ, "gy", "gx", None)
    return jax.shard_map(
        per_device,
        mesh=mesh,
        in_specs=(grid, P(), P(), P(), P(), P(), P(), grid),
        out_specs=(grid, P(), P(), P(), P(), P(), P()),
        check_vma=False,
    )
```
